32 devices in a mesh: grp: 2 (over y), segment: 2 (over core), row: 4 (over z), col: 2 (over x).
Axes of the slice: x: 2, y: 2, z: 4, core: 2. Of those that a mesh axis runs over, the one named last changes fastest.
Arguments:
- latent: bfloat16 [4, 16, 128, 320], P('grp', 'row', 'col'), parts along dimension 0, may hold values from -6 to 6
- enc_first: bfloat16 [9, 320, 320], P(None, None, 'row'), may hold values from -0.15625 to 0.15625
- enc_first_bias: float32 [320], replicated, may hold values from -3 to 3
- enc_second: bfloat16 [9, 320, 320], P(None, None, 'row'), may hold values from -0.15625 to 0.15625
- enc_second_bias: float32 [320], replicated, may hold values from -3 to 3
- mid_weight: bfloat16 [9, 320, 640], P(None, None, 'row'), may hold values from -0.15625 to 0.15625
- mid_bias: float32 [640], replicated, may hold values from -3 to 3
- dec_first: bfloat16 [9, 960, 320], P(None, None, 'row'), may hold values from -0.09375 to 0.09375
- dec_first_bias: float32 [320], replicated, may hold values from -3 to 3
- dec_second: bfloat16 [9, 320, 320], P(None, None, 'row'), may hold values from -0.15625 to 0.15625
- dec_second_bias: float32 [320], replicated, may hold values from -3 to 3
Outputs:
- decoded: bfloat16 [4, 16, 128, 320], P(('grp', 'segment'), 'row', 'col'), parts along dimension 0
The draws below stay inside these ranges and needn't reach their ends.
There are 2 independent parts, one for each index of `grp`. The reference program is written for one: setup_inputs(seed, part) draws one part's arguments, and reference() takes and returns one part's arrays. A program takes and returns all parts, laid end to end along the dimension named above; an argument that names none is the same for every part. Nothing has to cross between parts.
All inputs are finite; a program needn't handle non-finite values.
Results may differ from the reference program's by a relative error of at most 0.0075.
Values may be sent and summed in bfloat16 or wider, within the bound.
No kernel may reach another device: no remote copies, remote signals or barrier semaphores. Data moves between devices by JAX's collectives and lax.ppermute only.
A program may use at most 128 MiB of HBM per device.

```python
import jax
import jax.numpy as jnp

C1 = 320
C2 = 640
MB = 2
HEIGHT = 16
WIDTH = 128


def levels(key, dims, split, low, high):
    def one(axis_at, parts):
        draws = jax.random.uniform(jax.random.fold_in(jax.random.fold_in(key, 6), axis_at), (parts,), jnp.float32, low / len(split), high / len(split))
        return jnp.repeat(jnp.exp(draws), dims[axis_at] // parts).reshape((-1,) + (1,) * (len(dims) - axis_at - 1))

    gain = one(*split[0])
    for cut in split[1:]:
        gain = gain * one(*cut)
    return gain


def gaussian(stream_key, shape, scale, reach, cuts=(), dtype=jnp.bfloat16):
    gain = levels(stream_key, shape, cuts, -0.22, 0.18) if cuts else 1.0
    result = jax.random.normal(stream_key, shape, jnp.float32) * scale * gain
    return jnp.minimum(jnp.maximum(result, -reach), reach).astype(dtype)


def setup_inputs(seed: int = 0, part: int = 0) -> dict:
    key_of = jax.random.split(jax.random.key(seed), 12)
    part_keys = jax.random.split(jax.random.fold_in(key_of[11], part), 12)
    latent = gaussian(part_keys[0], (MB, HEIGHT, WIDTH, C1), 1.0, 6.0, ((1, 4), (2, 2)))
    enc_first = gaussian(key_of[1], (9, C1, C1), (4 * C1) ** -0.5, 0.15625, ((2, 4),))
    enc_first_bias = gaussian(key_of[2], (C1,), 0.5, 3.0, (), jnp.float32)
    enc_second = gaussian(key_of[3], (9, C1, C1), (4 * C1) ** -0.5, 0.15625, ((2, 4),))
    enc_second_bias = gaussian(key_of[4], (C1,), 0.5, 3.0, (), jnp.float32)
    mid_weight = gaussian(key_of[5], (9, C1, C2), (4 * C1) ** -0.5, 0.15625, ((2, 4),))
    mid_bias = gaussian(key_of[6], (C2,), 0.5, 3.0, (), jnp.float32)
    dec_first = gaussian(key_of[7], (9, C1 + C2, C1), (4 * (C1 + C2)) ** -0.5, 0.09375, ((2, 4),))
    dec_first_bias = gaussian(key_of[8], (C1,), 0.5, 3.0, (), jnp.float32)
    dec_second = gaussian(key_of[9], (9, C1, C1), (4 * C1) ** -0.5, 0.15625, ((2, 4),))
    dec_second_bias = gaussian(key_of[10], (C1,), 0.5, 3.0, (), jnp.float32)
    return {"latent": latent, "enc_first": enc_first, "enc_first_bias": enc_first_bias, "enc_second": enc_second, "enc_second_bias": enc_second_bias, "mid_weight": mid_weight, "mid_bias": mid_bias, "dec_first": dec_first, "dec_first_bias": dec_first_bias, "dec_second": dec_second, "dec_second_bias": dec_second_bias}


def conv_layer(inputs, weight, bias):
    rows, cols = inputs.shape[1], inputs.shape[2]
    padded = jnp.pad(inputs, ((0, 0), (1, 1), (1, 1), (0, 0)))
    total = jnp.zeros(inputs.shape[:3] + (weight.shape[2],), jnp.float32)
    for tap in range(9):
        shift_row, shift_col = tap // 3, tap % 3
        window = padded[:, shift_row:shift_row + rows, shift_col:shift_col + cols, :]
        total = total + jnp.einsum("brck,kn->brcn", window.astype(jnp.float32), weight[tap].astype(jnp.float32))
    return jax.nn.silu(total + bias.astype(jnp.float32)).astype(jnp.bfloat16)


def pool_cells(inputs):
    batch, rows, cols, chans = inputs.shape
    blocks = inputs.astype(jnp.float32).reshape(batch, rows // 2, 2, cols // 2, 2, chans)
    return jnp.mean(blocks, axis=(2, 4)).astype(jnp.bfloat16)


def reference(latent, enc_first, enc_first_bias, enc_second, enc_second_bias, mid_weight, mid_bias, dec_first, dec_first_bias, dec_second, dec_second_bias):
    hidden = conv_layer(latent, enc_first, enc_first_bias)
    skip = conv_layer(hidden, enc_second, enc_second_bias)
    middle = conv_layer(pool_cells(skip), mid_weight, mid_bias)
    upsampled = jnp.repeat(jnp.repeat(middle, 2, axis=1), 2, axis=2)
    joined = jnp.concatenate([skip, upsampled], axis=3)
    refined = conv_layer(joined, dec_first, dec_first_bias)
    return conv_layer(refined, dec_second, dec_second_bias)
```

```python
import functools

import jax
import jax.numpy as jnp
from jax import lax
from jax.experimental import pallas as pl
from jax.experimental.pallas import tpu as pltpu
from jax.sharding import PartitionSpec as P

BF = jnp.bfloat16
F32 = jnp.float32
LANES = 128
SIDE = 8
AXES = ("grp", "segment", "row", "col")
PIECES = 8
SHARDS = 4
VMEM = pl.BlockSpec(memory_space=pltpu.VMEM)
HBM = pl.BlockSpec(memory_space=pl.ANY)
SMEM = pl.BlockSpec(memory_space=pltpu.SMEM)


def params():
    return pltpu.CompilerParams(vmem_limit_bytes=52 * 1024 * 1024)


def plain_chunks(base):
    chunks = [[(tap, base + half * LANES, LANES)] for tap in range(9) for half in range(2)]
    rest = [(tap, base + 256, 64) for tap in range(9)]
    for at in range(0, 9, 2):
        chunks.append(rest[at : at + 2])
    return chunks


def joined_chunks():
    chunks = plain_chunks(0)
    for tap in range(9):
        for shard in range(4):
            chunks.append([(tap, 320 + shard * 160, LANES)])
        chunks.append([(tap, 320 + shard * 160 + LANES, 32) for shard in range(4)])
    return chunks


def padded_count(chunks):
    return -(-len(chunks) // PIECES) * PIECES


def pack_body(layouts, *refs):
    count = len(layouts)
    for chunks, source, target in zip(layouts, refs[:count], refs[count:]):
        channels = source.shape[2]
        for index in range(target.shape[0]):
            if index < len(chunks):
                parts = [source[tap, pl.ds(first, size), :] for tap, first, size in chunks[index]]
                have = sum(part.shape[0] for part in parts)
                if have < LANES:
                    parts.append(jnp.zeros((LANES - have, channels), BF))
                block = parts[0] if len(parts) == 1 else jnp.concatenate(parts, axis=0)
                target[index] = block.T
            else:
                target[index] = jnp.zeros((channels, LANES), BF)


def pack(layouts, weights):
    shapes = [
        jax.ShapeDtypeStruct((padded_count(chunks), weight.shape[2], LANES), BF)
        for chunks, weight in zip(layouts, weights)
    ]
    return pl.pallas_call(
        functools.partial(pack_body, layouts),
        out_shape=shapes,
        in_specs=[VMEM] * len(weights),
        out_specs=[VMEM] * len(weights),
        compiler_params=params(),
        name="pack_weights",
    )(*weights)


def device_pairs(mesh_shape, move):
    grps, segs, rows, cols = mesh_shape
    place = lambda g, s, r, c: ((g * segs + s) * rows + r) * cols + c
    return [
        (place(g, s, r, c), place(*move(g, s, r, c)))
        for g in range(grps)
        for s in range(segs)
        for r in range(rows)
        for c in range(cols)
    ]


def cyclic(count, by):
    return [(i, (i + by) % count) for i in range(count)]


def gather_planes(packed, piece, count):
    size = packed.shape[0] // PIECES
    mine = lax.dynamic_slice_in_dim(packed, piece * size, size, axis=0)
    return jnp.concatenate(
        [lax.ppermute(mine, "row", cyclic(count, by)) for by in range(1, count)], axis=0
    )


def gather_plane(block, mesh_shape):
    first = device_pairs(
        mesh_shape, lambda g, s, r, c: (g, s, r, 1 - c) if s == 0 else (1 - g, s, r, c)
    )
    second = device_pairs(
        mesh_shape, lambda g, s, r, c: (1 - g, s, r, c) if s == 0 else (g, s, r, 1 - c)
    )
    block = jnp.concatenate([block, lax.ppermute(block, AXES, first)], axis=0)
    block = jnp.concatenate([block, lax.ppermute(block, AXES, second)], axis=0)
    return block, lax.ppermute(block, "segment", [(0, 1), (1, 0)])


def load_weights(place, sources, target, sem):
    if len(sources) == 1:
        return [pltpu.make_async_copy(sources[0], target, sem)]
    own, near, far = sources
    grp, seg, row, col = (place[i] for i in range(4))
    size = own.shape[0] // PIECES
    copies = [pltpu.make_async_copy(own, target.at[:, row], sem)]
    for part, core in ((near, seg), (far, 1 - seg)):
        for slot in range(4):
            low, high = slot % 2, slot // 2
            flip_col = jnp.where(core == 0, low, high)
            flip_grp = jnp.where(core == 0, high, low)
            owner_grp = jnp.where(flip_grp == 1, 1 - grp, grp)
            owner_col = jnp.where(flip_col == 1, 1 - col, col)
            piece = (owner_grp * 2 + core) * 2 + owner_col
            for by in range(1, SHARDS):
                shard = lax.rem(row - by + SHARDS, SHARDS)
                source = part.at[pl.ds((slot * 3 + by - 1) * size, size)]
                copies.append(
                    pltpu.make_async_copy(source, target.at[pl.ds(piece * size, size), shard], sem)
                )
    return copies


def silu(value):
    return value / (1.0 + jnp.exp(-value))


def spread(value, shifted):
    cells = value.shape[0]
    shifted[0, :cells] = pltpu.roll(value, 1, 0).astype(BF)
    shifted[1, :cells] = value.astype(BF)
    shifted[2, :cells] = pltpu.roll(value, cells - 1, 0).astype(BF)


def weight_pair(weights, low, high):
    parts = []
    for index in (low, high):
        if index is not None:
            block = weights[index]
            parts.append(block.reshape(block.shape[0] * block.shape[1], LANES))
    return parts[0] if len(parts) == 1 else jnp.concatenate(parts, axis=1)


def product(left, right):
    return lax.dot_general(left, right, (((1,), (1,)), ((), ())), preferred_element_type=F32)


def add_plain(shifted, weights, rows, wide, acc, bias):
    cells = rows * wide

    def window(tap, first, size):
        at = (tap // 3) * wide
        return shifted[tap % 3, pl.ds(at, cells), pl.ds(first, size)]

    def rest(at):
        low = window(2 * at, 256, LANES)
        if at == 4:
            return low
        high = window(2 * at + 1, 256, LANES)
        lane = lax.broadcasted_iota(jnp.int32, (cells, LANES), 1)
        return jnp.where(lane < 64, low, high)

    acc[:cells] = product(window(0, 0, 256), weight_pair(weights, 0, 1)) + bias
    for tap in range(1, 9):
        acc[:cells] += product(window(tap, 0, 256), weight_pair(weights, 2 * tap, 2 * tap + 1))
    for at in range(0, 4, 2):
        left = jnp.concatenate([rest(at), rest(at + 1)], axis=1)
        acc[:cells] += product(left, weight_pair(weights, 18 + at, 19 + at))
    acc[:cells] += product(rest(4), weight_pair(weights, 22, None))


def inside(place, rows, wide, first_row, first_col, size):
    tile_rows, tile_cols, row_count, col_count = size
    row = lax.broadcasted_iota(jnp.int32, (rows, wide, 1), 0) + (place[2] * tile_rows + first_row)
    col = lax.broadcasted_iota(jnp.int32, (rows, wide, 1), 1) + (place[3] * tile_cols + first_col)
    return (row >= 0) & (row < tile_rows * row_count) & (col >= 0) & (col < tile_cols * col_count)


def activated(acc, rows, wide, keep):
    value = silu(acc[: rows * wide]).reshape(rows, wide, acc.shape[1])
    value = jnp.where(keep, value, 0.0).reshape(rows * wide, acc.shape[1])
    value = value.astype(BF).astype(F32)
    return jnp.concatenate([value, value[:, 256:320]], axis=1)


def encoder_body(size, sets, place, cells, bias1, bias2, *refs):
    tile_rows, tile_cols = size[:2]
    wide = tile_cols + 2 * SIDE
    sources1, refs = refs[:sets], refs[sets:]
    sources2, refs = refs[:sets], refs[sets:]
    skip, pooled, w1, w2, shifted, acc, sems = refs
    copies1 = load_weights(place, sources1, w1, sems.at[0])
    copies2 = load_weights(place, sources2, w2, sems.at[1])
    for copy in copies1 + copies2:
        copy.start()
    spread(cells[...].astype(F32), shifted)
    for copy in copies1:
        copy.wait()
    rows = tile_rows + 6
    add_plain(shifted, w1, rows, wide, acc, bias1[...])
    hidden = activated(acc, rows, wide, inside(place, rows, wide, -3, -SIDE, size))
    spread(hidden, shifted)
    for copy in copies2:
        copy.wait()
    rows = tile_rows + 4
    add_plain(shifted, w2, rows, wide, acc, bias2[...])
    value = activated(acc, rows, wide, inside(place, rows, wide, -2, -SIDE, size)).astype(BF)
    skip[...] = value
    half = pooled.shape[1]
    cell = lax.broadcasted_iota(jnp.int32, (half, 2 * wide), 1)
    cell = jnp.where(cell >= wide, cell - wide, cell)
    target = lax.broadcasted_iota(jnp.int32, (half, 2 * wide), 0)
    mean = jnp.where(cell // 2 == target, 0.25, 0.0).astype(BF)
    for row in range(tile_rows // 2):
        at = (2 + 2 * row) * wide
        block = value[at : at + 2 * wide]
        pooled[row] = jnp.dot(mean, block, preferred_element_type=F32).astype(BF)


def middle_body(size, place, own, *refs):
    tile_rows, tile_cols, row_count, col_count = size
    others, refs = refs[: row_count - 1], refs[row_count - 1 :]
    weights, bias = refs[:2]
    outs, refs = refs[2 : 2 + row_count], refs[2 + row_count :]
    field, shifted, acc, result = refs
    row = place[2]
    tall, half = tile_rows // 2, own.shape[1]
    rows = tall * row_count
    flat = (rows + 2) * half
    field[0] = jnp.zeros_like(field[0])
    field[rows + 1] = jnp.zeros_like(field[0])
    for by in range(row_count):
        source = own if by == 0 else others[by - 1]
        at = lax.rem(row - by + row_count, row_count)
        field[pl.ds(1 + tall * at, tall)] = source[...].astype(F32)
    spread(field[...].reshape(flat, field.shape[2]), shifted)
    cells = rows * half
    channels = weights.shape[2]
    acc[...] = jnp.zeros_like(acc)
    for tap in range(9):
        at = (tap // 3) * half
        left = shifted[tap % 3, pl.ds(at, cells), :]
        part = jnp.dot(left[:, :256], weights[tap, :256, :], preferred_element_type=F32)
        part += jnp.dot(left[:, 256:320], weights[tap, 256:320, :], preferred_element_type=F32)
        if tap == 0:
            part += bias[...]
        acc[:, :channels] += part
    col = lax.broadcasted_iota(jnp.int32, (rows, half, 1), 1)
    col = col + (place[3] * (tile_cols // 2) - SIDE // 2)
    keep = (col >= 0) & (col < tile_cols // 2 * col_count)
    value = silu(acc[...]).reshape(rows, half, 2 * LANES)
    value = jnp.where(keep, value, 0.0).reshape(cells, 2 * LANES)
    tail = pltpu.roll(value[:, LANES:], row * 32, 1)
    value = jnp.concatenate([value[:, :LANES], tail], axis=1).astype(BF)
    result[0] = jnp.zeros_like(result[0])
    result[rows + 1] = jnp.zeros_like(result[0])
    result[1 : rows + 1] = value.reshape(rows, half, 2 * LANES)
    for by in range(row_count):
        at = lax.rem(row + by, row_count)
        outs[by][...] = result[pl.ds(tall * at, tall + 2)]


def decoder_body(size, sets, place, skip, bias1, bias2, *refs):
    tile_rows, tile_cols = size[:2]
    wide = tile_cols + 2 * SIDE
    mids, refs = refs[:SHARDS], refs[SHARDS:]
    sources1, refs = refs[:sets], refs[sets:]
    sources2, refs = refs[:sets], refs[sets:]
    out, w1, w2, shifted, raised, field, acc, sems = refs
    copies1 = load_weights(place, sources1, w1, sems.at[0])
    copies2 = load_weights(place, sources2, w2, sems.at[1])
    for copy in copies1 + copies2:
        copy.start()
    spread(skip[...].astype(F32), shifted)
    half = mids[0].shape[1]
    tall = tile_rows // 2 + 2
    tail = mids[0][:, :, LANES:]
    for mid in mids[1:]:
        tail = tail + mid[:, :, LANES:]
    field[4] = tail
    for by in range(SHARDS):
        shard = lax.rem(place[2] - by + SHARDS, SHARDS) if sets == 3 else by
        field[shard] = mids[by][:, :, :LANES]
    cell = lax.broadcasted_iota(jnp.int32, (3 * wide, half), 0)
    move = jnp.where(cell >= 2 * wide, 1 - 2 * wide, jnp.where(cell >= wide, -wide, -1))
    source = lax.broadcasted_iota(jnp.int32, (3 * wide, half), 1)
    place_of = cell + move
    raise_by = jnp.where((place_of >= 2 * source) & (place_of < 2 * source + 2), 1.0, 0.0).astype(BF)
    for row in range(tall):
        block = jnp.concatenate([field[chunk, row] for chunk in range(5)], axis=1)
        up = jnp.dot(raise_by, block, preferred_element_type=F32).astype(BF)
        for dx in range(3):
            for twice in range(2):
                at = (2 * row + twice) * wide
                raised[dx, at : at + wide] = up[dx * wide : (dx + 1) * wide]
    for copy in copies1:
        copy.wait()
    rows = tile_rows + 2
    cells = rows * wide
    add_plain(shifted, w1, rows, wide, acc, bias1[...])

    def window(tap, first, count):
        return raised[tap % 3, pl.ds((tap // 3) * wide, cells), pl.ds(first, count)]

    for tap in range(9):
        at = 23 + 5 * tap
        for pair in range(2):
            left = window(tap, 256 * pair, 256)
            acc[:cells] += product(left, weight_pair(w1, at + 2 * pair, at + 2 * pair + 1))
        if tap % 2 == 1:
            left = jnp.concatenate([window(tap - 1, 512, LANES), window(tap, 512, LANES)], axis=1)
            acc[:cells] += product(left, weight_pair(w1, at - 1, at + 4))
        elif tap == 8:
            acc[:cells] += product(window(tap, 512, LANES), weight_pair(w1, at + 4, None))
    refined = activated(acc, rows, wide, inside(place, rows, wide, -1, -SIDE, size))
    spread(refined, shifted)
    for copy in copies2:
        copy.wait()
    add_plain(shifted, w2, tile_rows, wide, acc, bias2[...])
    value = silu(acc[: tile_rows * wide]).reshape(tile_rows, wide, acc.shape[1])
    out[0] = value[:, SIDE : SIDE + tile_cols, :].astype(BF)


def shards(mesh_shape, latent, enc_first, enc_first_bias, enc_second, enc_second_bias, mid_weight, mid_bias,
           dec_first, dec_first_bias, dec_second, dec_second_bias):
    grps, segs, row_count, col_count = mesh_shape
    grp, seg, row, col = (lax.axis_index(axis) for axis in AXES)
    place = jnp.stack([grp, seg, row, col]).astype(jnp.int32)
    piece = (grp * 2 + seg) * 2 + col
    tile_rows, tile_cols, channels = latent.shape[1:]
    size = (tile_rows, tile_cols, row_count, col_count)
    wide = tile_cols + 2 * SIDE
    half = -(-(wide // 2) // 16) * 16
    spread_out = row_count == SHARDS and col_count == 2 and grps == 2 and segs == 2
    plain, joined = plain_chunks(0), joined_chunks()

    if spread_out:
        (own1,) = pack((plain,), (enc_first,))
        (own2,) = pack((plain,), (enc_second,))
        own3, own4 = pack((joined, plain), (dec_first, dec_second))
        sets = 3
        weights = []
        for own in (own1, own2, own3, own4):
            block = gather_planes(own, piece, row_count)
            weights.append((own,) + gather_plane(block, mesh_shape))
    else:
        sets = 1
        weights = []
        for chunks, weight in ((plain, enc_first), (plain, enc_second), (joined, dec_first), (plain, dec_second)):
            full = lax.all_gather(weight, "row", axis=2, tiled=True)
            (own,) = pack((chunks,), (full,))
            weights.append((own.reshape(own.shape[0], SHARDS, -1, LANES),))

    tile = lax.dynamic_index_in_dim(latent, seg, 0, keepdims=False)
    down = [(i, i + 1) for i in range(row_count - 1)]
    above = lax.ppermute(tile, "row", down)
    below = lax.ppermute(tile, "row", [(b, a) for a, b in down])
    tile = jnp.concatenate([above, tile, below], axis=0)
    left_edge, right_edge = tile[:, :SIDE], tile[:, tile_cols - SIDE :]
    if col_count == 2:
        edge = lax.ppermute(jnp.where(col == 0, right_edge, left_edge), "col", [(0, 1), (1, 0)])
        blank = jnp.zeros_like(edge)
        left, right = jnp.where(col == 0, blank, edge), jnp.where(col == 0, edge, blank)
    else:
        along = [(i, i + 1) for i in range(col_count - 1)]
        left = lax.ppermute(right_edge, "col", along)
        right = lax.ppermute(left_edge, "col", [(b, a) for a, b in along])
    tile = jnp.concatenate([left, tile, right], axis=1)
    cells = jnp.concatenate([tile, tile[:, :, 256:]], axis=2).reshape(-1, 3 * LANES)

    scratch = lambda *shape: pltpu.VMEM(shape, BF)
    lines = lambda bias: bias.reshape(1, -1)
    skip, pooled = pl.pallas_call(
        functools.partial(encoder_body, size, sets),
        out_shape=[
            jax.ShapeDtypeStruct(((tile_rows + 4) * wide, 3 * LANES), BF),
            jax.ShapeDtypeStruct((tile_rows // 2, half, 3 * LANES), BF),
        ],
        in_specs=[SMEM, VMEM, VMEM, VMEM] + [HBM] * (2 * sets),
        out_specs=[VMEM, VMEM],
        scratch_shapes=[
            scratch(24, SHARDS, channels // SHARDS, LANES),
            scratch(24, SHARDS, channels // SHARDS, LANES),
            scratch(3, 3 * tile_rows * wide, 3 * LANES),
            pltpu.VMEM(((tile_rows + 6) * wide, channels), F32),
            pltpu.SemaphoreType.DMA((2,)),
        ],
        compiler_params=params(),
        name="encoder",
    )(place, cells, lines(enc_first_bias), lines(enc_second_bias), *weights[0], *weights[1])

    tall = tile_rows // 2
    if spread_out:
        others = [lax.ppermute(pooled, "row", cyclic(row_count, by)) for by in range(1, row_count)]
        part = mid_weight.shape[2]
        bias = lax.dynamic_slice_in_dim(mid_bias, row * part, part, 0)
        rows = tall * row_count
        sent = pl.pallas_call(
            functools.partial(middle_body, size),
            out_shape=[jax.ShapeDtypeStruct((tall + 2, half, 2 * LANES), BF)] * row_count,
            in_specs=[SMEM] + [VMEM] * (row_count + 2),
            out_specs=[VMEM] * row_count,
            scratch_shapes=[
                pltpu.VMEM((rows + 2, half, 3 * LANES), F32),
                scratch(3, (rows + 2) * half, 3 * LANES),
                pltpu.VMEM((rows * half, 2 * LANES), F32),
                scratch(rows + 2, half, 2 * LANES),
            ],
            compiler_params=params(),
            name="middle",
        )(place, pooled, *others, mid_weight, lines(bias))
        mids = [sent[0]] + [
            lax.ppermute(sent[by], "row", cyclic(row_count, by)) for by in range(1, row_count)
        ]
    else:
        full = lax.all_gather(mid_weight, "row", axis=2, tiled=True)
        field = jnp.concatenate(
            [lax.ppermute(pooled, "row", down), pooled, lax.ppermute(pooled, "row", [(b, a) for a, b in down])]
        )[:, :, :channels]
        field = jnp.pad(field, ((0, 0), (1, 1), (0, 0)))
        total = jnp.zeros((tall + 2, half, full.shape[2]), F32)
        first = field.shape[0] // 2 - tall // 2 - 2
        for tap in range(9):
            dy, dx = tap // 3, tap % 3
            window = field[first + dy : first + dy + tall + 2, dx : dx + half]
            total += jnp.einsum("rck,kn->rcn", window, full[tap], preferred_element_type=F32)
        at_row = jnp.arange(tall + 2)[:, None, None] - 1 + row * tall
        at_col = jnp.arange(half)[None, :, None] - SIDE // 2 + col * (tile_cols // 2)
        keep = (at_row >= 0) & (at_row < tall * row_count) & (at_col >= 0) & (at_col < tile_cols // 2 * col_count)
        middle = jnp.where(keep, jax.nn.silu(total + mid_bias), 0.0).astype(BF)
        mids = []
        for shard in range(SHARDS):
            block = middle[:, :, 160 * shard : 160 * (shard + 1)]
            tail = jnp.pad(block[:, :, LANES:], ((0, 0), (0, 0), (32 * shard, 96 - 32 * shard)))
            mids.append(jnp.concatenate([block[:, :, :LANES], tail], axis=2))

    return pl.pallas_call(
        functools.partial(decoder_body, size, sets),
        out_shape=jax.ShapeDtypeStruct((1, tile_rows, tile_cols, channels), BF),
        in_specs=[SMEM, VMEM, VMEM, VMEM] + [VMEM] * SHARDS + [HBM] * (2 * sets),
        out_specs=VMEM,
        scratch_shapes=[
            scratch(padded_count(joined), SHARDS, channels // SHARDS, LANES),
            scratch(24, SHARDS, channels // SHARDS, LANES),
            scratch(3, (tile_rows + 4) * wide, 3 * LANES),
            scratch(3, (tile_rows + 4) * wide, 5 * LANES),
            scratch(5, tall + 2, half, LANES),
            pltpu.VMEM(((tile_rows + 2) * wide, channels), F32),
            pltpu.SemaphoreType.DMA((2,)),
        ],
        compiler_params=params(),
        name="decoder",
    )(place, skip, lines(dec_first_bias), lines(dec_second_bias), *mids, *weights[2], *weights[3])


def solution(mesh):
    placed = (
        P("grp", "row", "col", None),
        P(None, None, "row"),
        P(),
        P(None, None, "row"),
        P(),
        P(None, None, "row"),
        P(),
        P(None, None, "row"),
        P(),
        P(None, None, "row"),
        P(),
    )
    mesh_shape = tuple(mesh.shape[axis] for axis in AXES)
    return jax.shard_map(
        functools.partial(shards, mesh_shape),
        mesh=mesh,
        in_specs=placed,
        out_specs=P(("grp", "segment"), "row", "col", None),
        check_vma=False,
    )
```

```python
import functools

import jax
import jax.numpy as jnp
from jax import lax
from jax.experimental import pallas as pl
from jax.experimental.pallas import tpu as pltpu
from jax.sharding import PartitionSpec as P

BF = jnp.bfloat16
F32 = jnp.float32
LANES = 128
SIDE = 8
AXES = ("grp", "segment", "row", "col")
PIECES = 8
SHARDS = 4
VMEM = pl.BlockSpec(memory_space=pltpu.VMEM)
HBM = pl.BlockSpec(memory_space=pl.ANY)
SMEM = pl.BlockSpec(memory_space=pltpu.SMEM)


def params():
    return pltpu.CompilerParams(vmem_limit_bytes=52 * 1024 * 1024)


def cost(cells):
    return pl.CostEstimate(flops=cells * 9 * 320 * 640 * 2, bytes_accessed=1 << 20, transcendentals=0)


def plain_chunks(base):
    chunks = [[(tap, base + half * LANES, LANES)] for tap in range(9) for half in range(2)]
    rest = [(tap, base + 256, 64) for tap in range(9)]
    for at in range(0, 9, 2):
        chunks.append(rest[at : at + 2])
    return chunks


def joined_chunks():
    chunks = plain_chunks(0)
    for tap in range(9):
        for shard in range(4):
            chunks.append([(tap, 320 + shard * 160, LANES)])
        chunks.append([(tap, 320 + shard * 160 + LANES, 32) for shard in range(4)])
    return chunks


def padded_count(chunks):
    return -(-len(chunks) // PIECES) * PIECES


def pack_body(layouts, parts, place, *refs):
    count = len(layouts)
    own, mine = refs[count:]
    index = 0
    for chunks, source in zip(layouts, refs):
        channels = source.shape[1]
        for chunk in chunks:
            parts = [source[tap, :, pl.ds(first, size)] for tap, first, size in chunk]
            have = sum(part.shape[1] for part in parts)
            if have < LANES:
                parts.append(jnp.zeros((channels, LANES - have), BF))
            own[index] = parts[0] if len(parts) == 1 else jnp.concatenate(parts, axis=1)
            index += 1
    while index < own.shape[0]:
        own[index] = jnp.zeros(own.shape[1:], BF)
        index += 1
    size = mine.shape[0]
    mine[...] = own[pl.ds(owner_piece(place, parts, place[1], 0) * size, size)]


def pack(layouts, parts, place, weights):
    total = padded_count([chunk for chunks in layouts for chunk in chunks])
    weights = [jnp.swapaxes(weight, 1, 2) for weight in weights]
    channels = weights[0].shape[1]
    return pl.pallas_call(
        functools.partial(pack_body, layouts, parts),
        out_shape=[
            jax.ShapeDtypeStruct((total, channels, LANES), BF),
            jax.ShapeDtypeStruct((total // parts, channels, LANES), BF),
        ],
        in_specs=[SMEM] + [VMEM] * len(weights),
        out_specs=[VMEM, VMEM],
        compiler_params=params(),
        name="pack_weights",
    )(place, *weights)


def device_pairs(mesh_shape, move):
    grps, segs, rows, cols = mesh_shape
    place = lambda g, s, r, c: ((g * segs + s) * rows + r) * cols + c
    return [
        (place(g, s, r, c), place(*move(g, s, r, c)))
        for g in range(grps)
        for s in range(segs)
        for r in range(rows)
        for c in range(cols)
    ]


def cyclic(count, by):
    return [(i, (i + by) % count) for i in range(count)]


def after(value, *others):
    return lax.optimization_barrier((value,) + others)[0]


def laid_body(cuts, *refs):
    count = len(cuts)
    sources, target, sems = refs[:count], refs[count], refs[count + 1]
    copies, at = [], 0
    for index, (source, (first, size)) in enumerate(zip(sources, cuts)):
        copies.append(
            pltpu.make_async_copy(
                source.at[pl.ds(first, size)], target.at[pl.ds(at, size)], sems.at[index]
            )
        )
        at += size
    for copy in copies:
        copy.start()
    for copy in copies:
        copy.wait()


def laid(*parts, cut=None):
    cuts = tuple(cut or (0, part.shape[0]) for part in parts)
    return pl.pallas_call(
        functools.partial(laid_body, cuts),
        out_shape=jax.ShapeDtypeStruct((sum(size for _, size in cuts),) + parts[0].shape[1:], BF),
        in_specs=[HBM] * len(parts),
        out_specs=VMEM,
        scratch_shapes=[pltpu.SemaphoreType.DMA((len(parts),))],
        compiler_params=params(),
        cost_estimate=pl.CostEstimate(flops=0, bytes_accessed=1 << 21, transcendentals=0),
        name="laid",
    )(*parts)


def from_planes(mine, count):
    return [lax.ppermute(mine, "row", cyclic(count, by)) for by in range(1, count)]


def plane_moves(mesh_shape):
    first = device_pairs(
        mesh_shape, lambda g, s, r, c: (g, s, r, 1 - c) if s == 0 else (1 - g, s, r, c)
    )
    second = device_pairs(
        mesh_shape, lambda g, s, r, c: (1 - g, s, r, c) if s == 0 else (g, s, r, 1 - c)
    )
    return first, second


def swap_cores(block):
    return lax.ppermute(block, "segment", [(0, 1), (1, 0)])


def owner_piece(place, parts, core, slot):
    grp, col = place[0], place[3]
    low, high = slot % 2, slot // 2
    if parts == 4:
        col, grp = (1 - col, 1 - grp) if low else (col, grp)
        return jnp.where(core == 0, col, 2 + grp)
    flip_col = jnp.where(core == 0, low, high)
    flip_grp = jnp.where(core == 0, high, low)
    grp = jnp.where(flip_grp == 1, 1 - grp, grp)
    col = jnp.where(flip_col == 1, 1 - col, col)
    return (grp * 2 + core) * 2 + col


def load_weights(place, parts, sources, target, sem):
    if len(sources) == 1:
        return [pltpu.make_async_copy(sources[0], target, sem)]
    own, near0, near1, far0, far1 = sources
    seg, row = place[1], place[2]
    size = own.shape[0] // parts
    each = parts // 4
    copies = [pltpu.make_async_copy(own, target.at[:, row], sem)]
    for pair, core in (((near0, near1), seg), ((far0, far1), 1 - seg)):
        for slot in range(2 * each):
            array = pair[slot // each]
            piece = owner_piece(place, parts, core, slot)
            for by in range(1, SHARDS):
                shard = lax.rem(row - by + SHARDS, SHARDS)
                source = array.at[pl.ds(((slot % each) * 3 + by - 1) * size, size)]
                copies.append(
                    pltpu.make_async_copy(source, target.at[pl.ds(piece * size, size), shard], sem)
                )
    return copies


def silu(value):
    return value / (1.0 + jnp.exp(-value))


def spread(value, shifted):
    cells = value.shape[0]
    shifted[0, :cells] = pltpu.roll(value, 1, 0).astype(BF)
    shifted[1, :cells] = value.astype(BF)
    shifted[2, :cells] = pltpu.roll(value, cells - 1, 0).astype(BF)


def weight_pair(weights, low, high):
    parts = []
    for index in (low, high):
        if index is not None:
            block = weights[index]
            parts.append(block.reshape(block.shape[0] * block.shape[1], LANES))
    return parts[0] if len(parts) == 1 else jnp.concatenate(parts, axis=1)


def product(left, right):
    return lax.dot_general(left, right, (((1,), (1,)), ((), ())), preferred_element_type=F32)


def add_plain(shifted, weights, base, rows, wide, acc, bias):
    cells = rows * wide

    def window(tap, first, size):
        at = (tap // 3) * wide
        return shifted[tap % 3, pl.ds(at, cells), pl.ds(first, size)]

    def rest(at):
        low = window(2 * at, 256, LANES)
        if at == 4:
            return low
        high = window(2 * at + 1, 256, LANES)
        lane = lax.broadcasted_iota(jnp.int32, (cells, LANES), 1)
        return jnp.where(lane < 64, low, high)

    acc[:cells] = product(window(0, 0, 256), weight_pair(weights, base, base + 1)) + bias
    for tap in range(1, 9):
        acc[:cells] += product(window(tap, 0, 256), weight_pair(weights, base + 2 * tap, base + 2 * tap + 1))
    for at in range(0, 4, 2):
        left = jnp.concatenate([rest(at), rest(at + 1)], axis=1)
        acc[:cells] += product(left, weight_pair(weights, base + 18 + at, base + 19 + at))
    acc[:cells] += product(rest(4), weight_pair(weights, base + 22, None))


def inside(place, rows, wide, first_row, first_col, size):
    tile_rows, tile_cols, row_count, col_count = size
    row = lax.broadcasted_iota(jnp.int32, (rows, wide, 1), 0) + (place[2] * tile_rows + first_row)
    col = lax.broadcasted_iota(jnp.int32, (rows, wide, 1), 1) + (place[3] * tile_cols + first_col)
    return (row >= 0) & (row < tile_rows * row_count) & (col >= 0) & (col < tile_cols * col_count)


def activated(acc, rows, wide, keep):
    value = silu(acc[: rows * wide]).reshape(rows, wide, acc.shape[1])
    value = jnp.where(keep, value, 0.0).reshape(rows * wide, acc.shape[1])
    value = value.astype(BF).astype(F32)
    return jnp.concatenate([value, value[:, 256:320]], axis=1)


def encoder_body(size, sets, parts, place, cells, bias1, bias2, *refs):
    tile_rows, tile_cols = size[:2]
    wide = tile_cols + 2 * SIDE
    sources, refs = refs[:sets], refs[sets:]
    skip, pooled, weights, shifted, acc, sem = refs
    copies = load_weights(place, parts, sources, weights, sem)
    for copy in copies:
        copy.start()
    spread(cells[...].astype(F32), shifted)
    for copy in copies:
        copy.wait()
    rows = tile_rows + 6
    add_plain(shifted, weights, 0, rows, wide, acc, bias1[...])
    hidden = activated(acc, rows, wide, inside(place, rows, wide, -3, -SIDE, size))
    spread(hidden, shifted)
    rows = tile_rows + 4
    add_plain(shifted, weights, 23, rows, wide, acc, bias2[...])
    value = activated(acc, rows, wide, inside(place, rows, wide, -2, -SIDE, size)).astype(BF)
    skip[...] = value
    half = pooled.shape[1]
    cell = lax.broadcasted_iota(jnp.int32, (half, 2 * wide), 1)
    cell = jnp.where(cell >= wide, cell - wide, cell)
    target = lax.broadcasted_iota(jnp.int32, (half, 2 * wide), 0)
    mean = jnp.where(cell // 2 == target, 0.25, 0.0).astype(BF)
    for row in range(tile_rows // 2):
        at = (2 + 2 * row) * wide
        block = value[at : at + 2 * wide]
        pooled[row] = jnp.dot(mean, block, preferred_element_type=F32).astype(BF)


def middle_body(size, place, own, *refs):
    tile_rows, tile_cols, row_count, col_count = size
    others, refs = refs[: row_count - 1], refs[row_count - 1 :]
    weights, bias = refs[:2]
    outs, refs = refs[2 : 2 + row_count], refs[2 + row_count :]
    field, shifted, acc, result = refs
    row = place[2]
    tall, half = tile_rows // 2, own.shape[1]
    rows = tall * row_count
    flat = (rows + 2) * half
    field[0] = jnp.zeros_like(field[0])
    field[rows + 1] = jnp.zeros_like(field[0])
    for by in range(row_count):
        source = own if by == 0 else others[by - 1]
        at = lax.rem(row - by + row_count, row_count)
        field[pl.ds(1 + tall * at, tall)] = source[...].astype(F32)
    spread(field[...].reshape(flat, field.shape[2]), shifted)
    cells = rows * half
    channels = weights.shape[1]
    acc[...] = jnp.zeros_like(acc)
    for tap in range(9):
        at = (tap // 3) * half
        left = shifted[tap % 3, pl.ds(at, cells), :]
        part = product(left[:, :256], weights[tap, :, :256])
        part += product(left[:, 256:320], weights[tap, :, 256:320])
        if tap == 0:
            part += bias[...]
        acc[:, :channels] += part
    col = lax.broadcasted_iota(jnp.int32, (rows, half, 1), 1)
    col = col + (place[3] * (tile_cols // 2) - SIDE // 2)
    keep = (col >= 0) & (col < tile_cols // 2 * col_count)
    value = silu(acc[...]).reshape(rows, half, 2 * LANES)
    value = jnp.where(keep, value, 0.0).reshape(cells, 2 * LANES)
    tail = pltpu.roll(value[:, LANES:], row * 32, 1)
    value = jnp.concatenate([value[:, :LANES], tail], axis=1).astype(BF)
    result[0] = jnp.zeros_like(result[0])
    result[rows + 1] = jnp.zeros_like(result[0])
    result[1 : rows + 1] = value.reshape(rows, half, 2 * LANES)
    for by in range(row_count):
        at = lax.rem(row + by, row_count)
        outs[by][...] = result[pl.ds(tall * at, tall + 2)]


def joined_body(size, sets, parts, place, skip, bias, *refs):
    tile_rows, tile_cols = size[:2]
    wide = tile_cols + 2 * SIDE
    mids, refs = refs[:SHARDS], refs[SHARDS:]
    sources, refs = refs[:sets], refs[sets:]
    out, weights, shifted, raised, field, acc, sem = refs
    copies = load_weights(place, parts, sources, weights, sem)
    for copy in copies:
        copy.start()
    spread(skip[...].astype(F32), shifted)
    half = mids[0].shape[1]
    tall = tile_rows // 2 + 2
    tail = mids[0][:, :, LANES:]
    for mid in mids[1:]:
        tail = tail + mid[:, :, LANES:]
    field[4] = tail
    for by in range(SHARDS):
        shard = lax.rem(place[2] - by + SHARDS, SHARDS) if sets > 1 else by
        field[shard] = mids[by][:, :, :LANES]
    cell = lax.broadcasted_iota(jnp.int32, (3 * wide, half), 0)
    move = jnp.where(cell >= 2 * wide, 1 - 2 * wide, jnp.where(cell >= wide, -wide, -1))
    source = lax.broadcasted_iota(jnp.int32, (3 * wide, half), 1)
    place_of = cell + move
    raise_by = jnp.where((place_of >= 2 * source) & (place_of < 2 * source + 2), 1.0, 0.0).astype(BF)
    for row in range(tall):
        block = jnp.concatenate([field[chunk, row] for chunk in range(5)], axis=1)
        up = jnp.dot(raise_by, block, preferred_element_type=F32).astype(BF)
        for dx in range(3):
            for twice in range(2):
                at = (2 * row + twice) * wide
                raised[dx, at : at + wide] = up[dx * wide : (dx + 1) * wide]
    for copy in copies:
        copy.wait()
    rows = tile_rows + 2
    cells = rows * wide
    add_plain(shifted, weights, 0, rows, wide, acc, bias[...])

    def window(tap, first, count):
        return raised[tap % 3, pl.ds((tap // 3) * wide, cells), pl.ds(first, count)]

    for tap in range(9):
        at = 23 + 5 * tap
        for pair in range(2):
            left = window(tap, 256 * pair, 256)
            acc[:cells] += product(left, weight_pair(weights, at + 2 * pair, at + 2 * pair + 1))
        if tap % 2 == 1:
            left = jnp.concatenate([window(tap - 1, 512, LANES), window(tap, 512, LANES)], axis=1)
            acc[:cells] += product(left, weight_pair(weights, at - 1, at + 4))
        elif tap == 8:
            acc[:cells] += product(window(tap, 512, LANES), weight_pair(weights, at + 4, None))
    out[...] = activated(acc, rows, wide, inside(place, rows, wide, -1, -SIDE, size)).astype(BF)


def last_body(size, sets, parts, place, refined, bias, *refs):
    tile_rows, tile_cols = size[:2]
    wide = tile_cols + 2 * SIDE
    sources, refs = refs[:sets], refs[sets:]
    out, weights, shifted, acc, sem = refs
    copies = load_weights(place, parts, sources, weights, sem)
    for copy in copies:
        copy.start()
    spread(refined[...].astype(F32), shifted)
    for copy in copies:
        copy.wait()
    add_plain(shifted, weights, 0, tile_rows, wide, acc, bias[...])
    value = silu(acc[...]).reshape(tile_rows, wide, acc.shape[1])
    out[0] = value[:, SIDE : SIDE + tile_cols, :].astype(BF)


def shards(mesh_shape, latent, enc_first, enc_first_bias, enc_second, enc_second_bias, mid_weight, mid_bias,
           dec_first, dec_first_bias, dec_second, dec_second_bias):
    grps, segs, row_count, col_count = mesh_shape
    grp, seg, row, col = (lax.axis_index(axis) for axis in AXES)
    place = jnp.stack([grp, seg, row, col]).astype(jnp.int32)
    tile_rows, tile_cols, channels = latent.shape[1:]
    size = (tile_rows, tile_cols, row_count, col_count)
    wide = tile_cols + 2 * SIDE
    half = -(-(wide // 2) // 16) * 16
    spread_out = row_count == SHARDS and col_count == 2 and grps == 2 and segs == 2
    plain, joined = plain_chunks(0), joined_chunks()

    groups = (
        ((plain, plain), 8, (enc_first, enc_second)),
        ((joined,), 8, (dec_first,)),
        ((plain,), 8, (dec_second,)),
    )
    if spread_out:
        (own0, mine0), (own1, mine1), (own2, mine2) = (
            pack(layouts, parts, place, group) for layouts, parts, group in groups
        )

    tile = lax.dynamic_index_in_dim(latent, seg, 0, keepdims=False)
    if spread_out:
        tile = after(tile, mine0)
    down = [(i, i + 1) for i in range(row_count - 1)]
    above = lax.ppermute(tile, "row", down)
    below = lax.ppermute(tile, "row", [(b, a) for a, b in down])
    tile = jnp.concatenate([above, tile, below], axis=0)
    left_edge, right_edge = tile[:, :SIDE], tile[:, tile_cols - SIDE :]
    if col_count == 2:
        edge = lax.ppermute(jnp.where(col == 0, right_edge, left_edge), "col", [(0, 1), (1, 0)])
        blank = jnp.zeros_like(edge)
        left, right = jnp.where(col == 0, blank, edge), jnp.where(col == 0, edge, blank)
    else:
        along = [(i, i + 1) for i in range(col_count - 1)]
        left = lax.ppermute(right_edge, "col", along)
        right = lax.ppermute(left_edge, "col", [(b, a) for a, b in along])
        edge = left
    tile = jnp.concatenate([left, tile, right], axis=1)
    cells = jnp.concatenate([tile, tile[:, :, 256:]], axis=2).reshape(-1, 3 * LANES)

    sets = 5 if spread_out else 1
    weights = []
    if spread_out:
        first, second = plane_moves(mesh_shape)
        across = lambda block, pairs: lax.ppermute(block, AXES, pairs)
        here0 = from_planes(mine0, row_count)
        here1 = from_planes(laid(mine1, mine2), row_count)
        block0 = laid(*here0)
        block0 = laid(block0, across(block0, first))
        block0 = after(block0, here1[0], above, below)
        far0 = swap_cores(block0)
        next0 = after(across(block0, second), edge, here1[1], here1[2])
        held0 = (block0, next0, far0, swap_cores(next0))
        part1, part2 = mine1.shape[0], mine2.shape[0]
        block1 = laid(*here1, cut=(0, part1))
        weights = [(own0,) + held0]
    else:
        for layouts, parts, group in groups:
            full = [lax.all_gather(weight, "row", axis=2, tiled=True) for weight in group]
            own = pack(layouts, parts, place, full)[0]
            weights.append((own.reshape(own.shape[0], SHARDS, -1, LANES),))

    scratch = lambda *shape: pltpu.VMEM(shape, BF)
    lines = lambda bias: bias.reshape(1, -1)
    packed = lambda source: scratch(source[0].shape[0], SHARDS, channels // SHARDS, LANES)
    skip, pooled = pl.pallas_call(
        functools.partial(encoder_body, size, sets, groups[0][1]),
        out_shape=[
            jax.ShapeDtypeStruct(((tile_rows + 4) * wide, 3 * LANES), BF),
            jax.ShapeDtypeStruct((tile_rows // 2, half, 3 * LANES), BF),
        ],
        in_specs=[SMEM, VMEM, VMEM, VMEM] + [HBM] * sets,
        out_specs=[VMEM, VMEM],
        scratch_shapes=[
            packed(weights[0]),
            scratch(3, 3 * tile_rows * wide, 3 * LANES),
            pltpu.VMEM(((tile_rows + 6) * wide, channels), F32),
            pltpu.SemaphoreType.DMA,
        ],
        compiler_params=params(),
        cost_estimate=cost(4 * (2 * tile_rows + 10) * wide),
        name="encoder",
    )(place, cells, lines(enc_first_bias), lines(enc_second_bias), *weights[0])

    tall = tile_rows // 2
    if spread_out:
        others = [lax.ppermute(pooled, "row", cyclic(row_count, by)) for by in range(1, row_count)]
        block1 = laid(block1, after(across(block1, first), pooled))
        far1 = swap_cores(block1)
        next1 = across(block1, second)
        block2 = laid(*here1, cut=(part1, part2))
        block2 = laid(block2, after(across(block2, first), pooled))
        others = after(others, block2)
        part = mid_weight.shape[2]
        bias = lax.dynamic_slice_in_dim(mid_bias, row * part, part, 0)
        rows = tall * row_count
        sent = pl.pallas_call(
            functools.partial(middle_body, size),
            out_shape=[jax.ShapeDtypeStruct((tall + 2, half, 2 * LANES), BF)] * row_count,
            in_specs=[SMEM] + [VMEM] * (row_count + 2),
            out_specs=[VMEM] * row_count,
            scratch_shapes=[
                pltpu.VMEM((rows + 2, half, 3 * LANES), F32),
                scratch(3, (rows + 2) * half, 3 * LANES),
                pltpu.VMEM((rows * half, 2 * LANES), F32),
                scratch(rows + 2, half, 2 * LANES),
            ],
            compiler_params=params(),
            cost_estimate=cost(4 * tile_rows * wide),
            name="middle",
        )(place, pooled, *others, jnp.swapaxes(mid_weight, 1, 2), lines(bias))
        mids = [sent[0]] + [
            lax.ppermute(sent[by], "row", cyclic(row_count, by)) for by in range(1, row_count)
        ]
        next1 = after(next1, sent[0])
        held1 = (block1, next1, far1, swap_cores(next1))
        next2 = after(across(after(block2, sent[0]), second), *mids)
        held2 = (block2, next2, swap_cores(block2), swap_cores(next2))
        weights += [(own1,) + held1, (own2,) + held2]
    else:
        full = lax.all_gather(mid_weight, "row", axis=2, tiled=True)
        field = jnp.concatenate(
            [lax.ppermute(pooled, "row", down), pooled, lax.ppermute(pooled, "row", [(b, a) for a, b in down])]
        )[:, :, :channels]
        field = jnp.pad(field, ((0, 0), (1, 1), (0, 0)))
        total = jnp.zeros((tall + 2, half, full.shape[2]), F32)
        first = field.shape[0] // 2 - tall // 2 - 2
        for tap in range(9):
            dy, dx = tap // 3, tap % 3
            window = field[first + dy : first + dy + tall + 2, dx : dx + half]
            total += jnp.einsum("rck,kn->rcn", window, full[tap], preferred_element_type=F32)
        at_row = jnp.arange(tall + 2)[:, None, None] - 1 + row * tall
        at_col = jnp.arange(half)[None, :, None] - SIDE // 2 + col * (tile_cols // 2)
        keep = (at_row >= 0) & (at_row < tall * row_count) & (at_col >= 0) & (at_col < tile_cols // 2 * col_count)
        middle = jnp.where(keep, jax.nn.silu(total + mid_bias), 0.0).astype(BF)
        mids = []
        for shard in range(SHARDS):
            block = middle[:, :, 160 * shard : 160 * (shard + 1)]
            tail = jnp.pad(block[:, :, LANES:], ((0, 0), (0, 0), (32 * shard, 96 - 32 * shard)))
            mids.append(jnp.concatenate([block[:, :, :LANES], tail], axis=2))

    refined = pl.pallas_call(
        functools.partial(joined_body, size, sets, groups[1][1]),
        out_shape=jax.ShapeDtypeStruct(((tile_rows + 2) * wide, 3 * LANES), BF),
        in_specs=[SMEM, VMEM, VMEM] + [VMEM] * SHARDS + [HBM] * sets,
        out_specs=VMEM,
        scratch_shapes=[
            packed(weights[1]),
            scratch(3, (tile_rows + 4) * wide, 3 * LANES),
            scratch(3, (tile_rows + 4) * wide, 5 * LANES),
            scratch(5, tall + 2, half, LANES),
            pltpu.VMEM(((tile_rows + 2) * wide, channels), F32),
            pltpu.SemaphoreType.DMA,
        ],
        compiler_params=params(),
        cost_estimate=cost(6 * (tile_rows + 2) * wide),
        name="joined",
    )(place, skip, lines(dec_first_bias), *mids, *weights[1])
    return pl.pallas_call(
        functools.partial(last_body, size, sets, groups[2][1]),
        out_shape=jax.ShapeDtypeStruct((1, tile_rows, tile_cols, channels), BF),
        in_specs=[SMEM, VMEM, VMEM] + [HBM] * sets,
        out_specs=VMEM,
        scratch_shapes=[
            packed(weights[2]),
            scratch(3, (tile_rows + 2) * wide, 3 * LANES),
            pltpu.VMEM((tile_rows * wide, channels), F32),
            pltpu.SemaphoreType.DMA,
        ],
        compiler_params=params(),
        cost_estimate=cost(2 * tile_rows * wide),
        name="last",
    )(place, refined, lines(dec_second_bias), *weights[2])


def solution(mesh):
    placed = (
        P("grp", "row", "col", None),
        P(None, None, "row"),
        P(),
        P(None, None, "row"),
        P(),
        P(None, None, "row"),
        P(),
        P(None, None, "row"),
        P(),
        P(None, None, "row"),
        P(),
    )
    mesh_shape = tuple(mesh.shape[axis] for axis in AXES)
    return jax.shard_map(
        functools.partial(shards, mesh_shape),
        mesh=mesh,
        in_specs=placed,
        out_specs=P(("grp", "segment"), "row", "col", None),
        check_vma=False,
    )
```

```python
import functools

import jax
import jax.numpy as jnp
from jax import lax
from jax.experimental import pallas as pl
from jax.experimental.pallas import tpu as pltpu
from jax.sharding import PartitionSpec as P

BF = jnp.bfloat16
F32 = jnp.float32
LANES = 128
SIDE = 8
AXES = ("grp", "segment", "row", "col")
PIECES = 8
SHARDS = 4
VMEM = pl.BlockSpec(memory_space=pltpu.VMEM)
HBM = pl.BlockSpec(memory_space=pl.ANY)
SMEM = pl.BlockSpec(memory_space=pltpu.SMEM)


def params():
    return pltpu.CompilerParams(vmem_limit_bytes=52 * 1024 * 1024)


def cost(cells):
    return pl.CostEstimate(flops=cells * 9 * 320 * 640 * 2, bytes_accessed=1 << 20, transcendentals=0)


def plain_chunks(base):
    chunks = [[(tap, base + half * LANES, LANES)] for tap in range(9) for half in range(2)]
    rest = [(tap, base + 256, 64) for tap in range(9)]
    for at in range(0, 9, 2):
        chunks.append(rest[at : at + 2])
    return chunks


def joined_chunks():
    chunks = plain_chunks(0)
    for tap in range(9):
        for shard in range(4):
            chunks.append([(tap, 320 + shard * 160, LANES)])
        chunks.append([(tap, 320 + shard * 160 + LANES, 32) for shard in range(4)])
    return chunks


def padded_count(chunks):
    return -(-len(chunks) // PIECES) * PIECES


def pack_body(layouts, parts, place, *refs):
    count = len(layouts)
    own, mine = refs[count:]
    index = 0
    for chunks, source in zip(layouts, refs):
        channels = source.shape[1]
        for chunk in chunks:
            parts = [source[tap, :, pl.ds(first, size)] for tap, first, size in chunk]
            have = sum(part.shape[1] for part in parts)
            if have < LANES:
                parts.append(jnp.zeros((channels, LANES - have), BF))
            own[index] = parts[0] if len(parts) == 1 else jnp.concatenate(parts, axis=1)
            index += 1
    while index < own.shape[0]:
        own[index] = jnp.zeros(own.shape[1:], BF)
        index += 1
    size = mine.shape[0]
    mine[...] = own[pl.ds(owner_piece(place, parts, place[1], 0) * size, size)]


def pack(layouts, parts, place, weights):
    total = padded_count([chunk for chunks in layouts for chunk in chunks])
    weights = [jnp.swapaxes(weight, 1, 2) for weight in weights]
    channels = weights[0].shape[1]
    return pl.pallas_call(
        functools.partial(pack_body, layouts, parts),
        out_shape=[
            jax.ShapeDtypeStruct((total, channels, LANES), BF),
            jax.ShapeDtypeStruct((total // parts, channels, LANES), BF),
        ],
        in_specs=[SMEM] + [VMEM] * len(weights),
        out_specs=[VMEM, VMEM],
        compiler_params=params(),
        name="pack_weights",
    )(place, *weights)


def device_pairs(mesh_shape, move):
    grps, segs, rows, cols = mesh_shape
    place = lambda g, s, r, c: ((g * segs + s) * rows + r) * cols + c
    return [
        (place(g, s, r, c), place(*move(g, s, r, c)))
        for g in range(grps)
        for s in range(segs)
        for r in range(rows)
        for c in range(cols)
    ]


def cyclic(count, by):
    return [(i, (i + by) % count) for i in range(count)]


def after(value, *others):
    return lax.optimization_barrier((value,) + others)[0]


def laid_body(cuts, *refs):
    count = len(cuts)
    sources, target, sems = refs[:count], refs[count], refs[count + 1]
    copies, at = [], 0
    for index, (source, (first, size)) in enumerate(zip(sources, cuts)):
        copies.append(
            pltpu.make_async_copy(
                source.at[pl.ds(first, size)], target.at[pl.ds(at, size)], sems.at[index]
            )
        )
        at += size
    for copy in copies:
        copy.start()
    for copy in copies:
        copy.wait()


def laid(*parts, cut=None):
    cuts = tuple(cut or (0, part.shape[0]) for part in parts)
    return pl.pallas_call(
        functools.partial(laid_body, cuts),
        out_shape=jax.ShapeDtypeStruct((sum(size for _, size in cuts),) + parts[0].shape[1:], BF),
        in_specs=[HBM] * len(parts),
        out_specs=VMEM,
        scratch_shapes=[pltpu.SemaphoreType.DMA((len(parts),))],
        compiler_params=params(),
        cost_estimate=pl.CostEstimate(flops=0, bytes_accessed=1 << 21, transcendentals=0),
        name="laid",
    )(*parts)


def from_planes(mine, count):
    return [lax.ppermute(mine, "row", cyclic(count, by)) for by in range(1, count)]


def plane_moves(mesh_shape):
    first = device_pairs(
        mesh_shape, lambda g, s, r, c: (g, s, r, 1 - c) if s == 0 else (1 - g, s, r, c)
    )
    second = device_pairs(
        mesh_shape, lambda g, s, r, c: (1 - g, s, r, c) if s == 0 else (g, s, r, 1 - c)
    )
    return first, second


def swap_cores(block):
    return lax.ppermute(block, "segment", [(0, 1), (1, 0)])


def owner_piece(place, parts, core, slot):
    grp, col = place[0], place[3]
    low, high = slot % 2, slot // 2
    if parts == 4:
        col, grp = (1 - col, 1 - grp) if low else (col, grp)
        return jnp.where(core == 0, col, 2 + grp)
    flip_col = jnp.where(core == 0, low, high)
    flip_grp = jnp.where(core == 0, high, low)
    grp = jnp.where(flip_grp == 1, 1 - grp, grp)
    col = jnp.where(flip_col == 1, 1 - col, col)
    return (grp * 2 + core) * 2 + col


def load_weights(place, parts, sources, target, sem):
    if len(sources) == 1:
        return [pltpu.make_async_copy(sources[0], target, sem)]
    own, near0, near1, far0, far1 = sources
    seg, row = place[1], place[2]
    size = own.shape[0] // parts
    each = parts // 4
    copies = [pltpu.make_async_copy(own, target.at[:, row], sem)]
    for pair, core in (((near0, near1), seg), ((far0, far1), 1 - seg)):
        for slot in range(2 * each):
            array = pair[slot // each]
            piece = owner_piece(place, parts, core, slot)
            for by in range(1, SHARDS):
                shard = lax.rem(row - by + SHARDS, SHARDS)
                source = array.at[pl.ds(((slot % each) * 3 + by - 1) * size, size)]
                copies.append(
                    pltpu.make_async_copy(source, target.at[pl.ds(piece * size, size), shard], sem)
                )
    return copies


def silu(value):
    return value / (1.0 + jnp.exp(-value))


def spread(value, shifted):
    cells = value.shape[0]
    shifted[0, :cells] = pltpu.roll(value, 1, 0).astype(BF)
    shifted[1, :cells] = value.astype(BF)
    shifted[2, :cells] = pltpu.roll(value, cells - 1, 0).astype(BF)


def weight_pair(weights, low, high):
    parts = []
    for index in (low, high):
        if index is not None:
            block = weights[index]
            parts.append(block.reshape(block.shape[0] * block.shape[1], LANES))
    return parts[0] if len(parts) == 1 else jnp.concatenate(parts, axis=1)


def product(left, right):
    return lax.dot_general(left, right, (((1,), (1,)), ((), ())), preferred_element_type=F32)


def add_plain(shifted, weights, base, rows, wide, acc, bias):
    cells = rows * wide

    def window(tap, first, size):
        at = (tap // 3) * wide
        return shifted[tap % 3, pl.ds(at, cells), pl.ds(first, size)]

    def rest(at):
        low = window(2 * at, 256, LANES)
        if at == 4:
            return low
        high = window(2 * at + 1, 256, LANES)
        lane = lax.broadcasted_iota(jnp.int32, (cells, LANES), 1)
        return jnp.where(lane < 64, low, high)

    acc[:cells] = product(window(0, 0, 256), weight_pair(weights, base, base + 1)) + bias
    for tap in range(1, 9):
        acc[:cells] += product(window(tap, 0, 256), weight_pair(weights, base + 2 * tap, base + 2 * tap + 1))
    for at in range(0, 4, 2):
        left = jnp.concatenate([rest(at), rest(at + 1)], axis=1)
        acc[:cells] += product(left, weight_pair(weights, base + 18 + at, base + 19 + at))
    acc[:cells] += product(rest(4), weight_pair(weights, base + 22, None))


def inside(place, rows, wide, first_row, first_col, size):
    tile_rows, tile_cols, row_count, col_count = size
    row = lax.broadcasted_iota(jnp.int32, (rows, wide, 1), 0) + (place[2] * tile_rows + first_row)
    col = lax.broadcasted_iota(jnp.int32, (rows, wide, 1), 1) + (place[3] * tile_cols + first_col)
    return (row >= 0) & (row < tile_rows * row_count) & (col >= 0) & (col < tile_cols * col_count)


def activated(acc, rows, wide, keep):
    value = silu(acc[: rows * wide]).reshape(rows, wide, acc.shape[1])
    value = jnp.where(keep, value, 0.0).reshape(rows * wide, acc.shape[1])
    value = value.astype(BF).astype(F32)
    return jnp.concatenate([value, value[:, 256:320]], axis=1)


def encoder_body(size, sets, parts, place, cells, bias1, bias2, *refs):
    tile_rows, tile_cols = size[:2]
    wide = tile_cols + 2 * SIDE
    sources, refs = refs[:sets], refs[sets:]
    skip, pooled, weights, shifted, acc, sem = refs
    copies = load_weights(place, parts, sources, weights, sem)
    for copy in copies:
        copy.start()
    spread(cells[...].astype(F32), shifted)
    for copy in copies:
        copy.wait()
    rows = tile_rows + 6
    add_plain(shifted, weights, 0, rows, wide, acc, bias1[...])
    hidden = activated(acc, rows, wide, inside(place, rows, wide, -3, -SIDE, size))
    spread(hidden, shifted)
    rows = tile_rows + 4
    add_plain(shifted, weights, 23, rows, wide, acc, bias2[...])
    value = activated(acc, rows, wide, inside(place, rows, wide, -2, -SIDE, size)).astype(BF)
    skip[...] = value
    half = pooled.shape[1]
    cell = lax.broadcasted_iota(jnp.int32, (half, 2 * wide), 1)
    cell = jnp.where(cell >= wide, cell - wide, cell)
    target = lax.broadcasted_iota(jnp.int32, (half, 2 * wide), 0)
    mean = jnp.where(cell // 2 == target, 0.25, 0.0).astype(BF)
    for row in range(tile_rows // 2):
        at = (2 + 2 * row) * wide
        block = value[at : at + 2 * wide]
        pooled[row] = jnp.dot(mean, block, preferred_element_type=F32).astype(BF)


def middle_body(size, place, own, *refs):
    tile_rows, tile_cols, row_count, col_count = size
    others, refs = refs[: row_count - 1], refs[row_count - 1 :]
    weights, bias = refs[:2]
    outs, refs = refs[2 : 2 + row_count], refs[2 + row_count :]
    field, shifted, acc, result = refs
    row = place[2]
    tall, half = tile_rows // 2, own.shape[1]
    rows = tall * row_count
    flat = (rows + 2) * half
    field[0] = jnp.zeros_like(field[0])
    field[rows + 1] = jnp.zeros_like(field[0])
    for by in range(row_count):
        source = own if by == 0 else others[by - 1]
        at = lax.rem(row - by + row_count, row_count)
        field[pl.ds(1 + tall * at, tall)] = source[...].astype(F32)
    spread(field[...].reshape(flat, field.shape[2]), shifted)
    cells = rows * half
    channels = weights.shape[1]
    acc[...] = jnp.zeros_like(acc)
    for tap in range(9):
        at = (tap // 3) * half
        left = shifted[tap % 3, pl.ds(at, cells), :]
        part = product(left[:, :256], weights[tap, :, :256])
        part += product(left[:, 256:320], weights[tap, :, 256:320])
        if tap == 0:
            part += bias[...]
        acc[:, :channels] += part
    col = lax.broadcasted_iota(jnp.int32, (rows, half, 1), 1)
    col = col + (place[3] * (tile_cols // 2) - SIDE // 2)
    keep = (col >= 0) & (col < tile_cols // 2 * col_count)
    value = silu(acc[...]).reshape(rows, half, 2 * LANES)
    value = jnp.where(keep, value, 0.0).reshape(cells, 2 * LANES)
    tail = pltpu.roll(value[:, LANES:], row * 32, 1)
    value = jnp.concatenate([value[:, :LANES], tail], axis=1).astype(BF)
    result[0] = jnp.zeros_like(result[0])
    result[rows + 1] = jnp.zeros_like(result[0])
    result[1 : rows + 1] = value.reshape(rows, half, 2 * LANES)
    for by in range(row_count):
        at = lax.rem(row + by, row_count)
        outs[by][...] = result[pl.ds(tall * at, tall + 2)]


def field_body(sets, place, *refs):
    mids, field = refs[:SHARDS], refs[SHARDS]
    tail = mids[0][:, :, LANES:]
    for mid in mids[1:]:
        tail = tail + mid[:, :, LANES:]
    field[4] = tail
    for by in range(SHARDS):
        shard = lax.rem(place[2] - by + SHARDS, SHARDS) if sets > 1 else by
        field[shard] = mids[by][:, :, :LANES]


def joined_body(size, sets, parts, place, skip, bias, *refs):
    tile_rows, tile_cols = size[:2]
    wide = tile_cols + 2 * SIDE
    field, refs = refs[0], refs[1:]
    sources, refs = refs[:sets], refs[sets:]
    out, weights, shifted, raised, acc, sem = refs
    copies = load_weights(place, parts, sources, weights, sem)
    for copy in copies:
        copy.start()
    spread(skip[...].astype(F32), shifted)
    half = field.shape[2]
    tall = tile_rows // 2 + 2
    cell = lax.broadcasted_iota(jnp.int32, (3 * wide, half), 0)
    move = jnp.where(cell >= 2 * wide, 1 - 2 * wide, jnp.where(cell >= wide, -wide, -1))
    source = lax.broadcasted_iota(jnp.int32, (3 * wide, half), 1)
    place_of = cell + move
    raise_by = jnp.where((place_of >= 2 * source) & (place_of < 2 * source + 2), 1.0, 0.0).astype(BF)
    for row in range(tall):
        block = jnp.concatenate([field[chunk, row] for chunk in range(5)], axis=1)
        up = jnp.dot(raise_by, block, preferred_element_type=F32).astype(BF)
        for dx in range(3):
            for twice in range(2):
                at = (2 * row + twice) * wide
                raised[dx, at : at + wide] = up[dx * wide : (dx + 1) * wide]
    for copy in copies:
        copy.wait()
    rows = tile_rows + 2
    cells = rows * wide
    add_plain(shifted, weights, 0, rows, wide, acc, bias[...])

    def window(tap, first, count):
        return raised[tap % 3, pl.ds((tap // 3) * wide, cells), pl.ds(first, count)]

    for tap in range(9):
        at = 23 + 5 * tap
        for pair in range(2):
            left = window(tap, 256 * pair, 256)
            acc[:cells] += product(left, weight_pair(weights, at + 2 * pair, at + 2 * pair + 1))
        if tap % 2 == 1:
            left = jnp.concatenate([window(tap - 1, 512, LANES), window(tap, 512, LANES)], axis=1)
            acc[:cells] += product(left, weight_pair(weights, at - 1, at + 4))
        elif tap == 8:
            acc[:cells] += product(window(tap, 512, LANES), weight_pair(weights, at + 4, None))
    out[...] = activated(acc, rows, wide, inside(place, rows, wide, -1, -SIDE, size)).astype(BF)


def last_body(size, sets, parts, place, refined, bias, *refs):
    tile_rows, tile_cols = size[:2]
    wide = tile_cols + 2 * SIDE
    sources, refs = refs[:sets], refs[sets:]
    out, weights, shifted, acc, sem = refs
    copies = load_weights(place, parts, sources, weights, sem)
    for copy in copies:
        copy.start()
    spread(refined[...].astype(F32), shifted)
    for copy in copies:
        copy.wait()
    add_plain(shifted, weights, 0, tile_rows, wide, acc, bias[...])
    value = silu(acc[...]).reshape(tile_rows, wide, acc.shape[1])
    out[0] = value[:, SIDE : SIDE + tile_cols, :].astype(BF)


def shards(mesh_shape, latent, enc_first, enc_first_bias, enc_second, enc_second_bias, mid_weight, mid_bias,
           dec_first, dec_first_bias, dec_second, dec_second_bias):
    grps, segs, row_count, col_count = mesh_shape
    grp, seg, row, col = (lax.axis_index(axis) for axis in AXES)
    place = jnp.stack([grp, seg, row, col]).astype(jnp.int32)
    tile_rows, tile_cols, channels = latent.shape[1:]
    size = (tile_rows, tile_cols, row_count, col_count)
    wide = tile_cols + 2 * SIDE
    half = -(-(wide // 2) // 16) * 16
    spread_out = row_count == SHARDS and col_count == 2 and grps == 2 and segs == 2
    plain, joined = plain_chunks(0), joined_chunks()

    groups = (
        ((plain, plain), 8, (enc_first, enc_second)),
        ((joined,), 8, (dec_first,)),
        ((plain,), 8, (dec_second,)),
    )
    if spread_out:
        (own0, mine0), (own1, mine1), (own2, mine2) = (
            pack(layouts, parts, place, group) for layouts, parts, group in groups
        )

    tile = lax.dynamic_index_in_dim(latent, seg, 0, keepdims=False)
    if spread_out:
        tile = after(tile, mine0)
    down = [(i, i + 1) for i in range(row_count - 1)]
    above = lax.ppermute(tile, "row", down)
    below = lax.ppermute(tile, "row", [(b, a) for a, b in down])
    tile = jnp.concatenate([above, tile, below], axis=0)
    left_edge, right_edge = tile[:, :SIDE], tile[:, tile_cols - SIDE :]
    if col_count == 2:
        edge = lax.ppermute(jnp.where(col == 0, right_edge, left_edge), "col", [(0, 1), (1, 0)])
        blank = jnp.zeros_like(edge)
        left, right = jnp.where(col == 0, blank, edge), jnp.where(col == 0, edge, blank)
    else:
        along = [(i, i + 1) for i in range(col_count - 1)]
        left = lax.ppermute(right_edge, "col", along)
        right = lax.ppermute(left_edge, "col", [(b, a) for a, b in along])
        edge = left
    tile = jnp.concatenate([left, tile, right], axis=1)
    cells = jnp.concatenate([tile, tile[:, :, 256:]], axis=2).reshape(-1, 3 * LANES)

    sets = 5 if spread_out else 1
    weights = []
    if spread_out:
        first, second = plane_moves(mesh_shape)
        across = lambda block, pairs: lax.ppermute(block, AXES, pairs)
        here0 = from_planes(mine0, row_count)
        late = laid(mine1, mine2)
        here1 = from_planes(late, row_count)
        block0 = laid(*after(here0, late))
        block0 = laid(block0, across(block0, first))
        block0 = after(block0, here1[0], above, below)
        far0 = swap_cores(block0)
        next0 = after(across(block0, second), edge, here1[1], here1[2])
        held0 = (block0, next0, far0, swap_cores(next0))
        part1, part2 = mine1.shape[0], mine2.shape[0]
        block1 = laid(*here1, cut=(0, part1))
        weights = [(own0,) + held0]
    else:
        for layouts, parts, group in groups:
            full = [lax.all_gather(weight, "row", axis=2, tiled=True) for weight in group]
            own = pack(layouts, parts, place, full)[0]
            weights.append((own.reshape(own.shape[0], SHARDS, -1, LANES),))

    scratch = lambda *shape: pltpu.VMEM(shape, BF)
    lines = lambda bias: bias.reshape(1, -1)
    packed = lambda source: scratch(source[0].shape[0], SHARDS, channels // SHARDS, LANES)
    skip, pooled = pl.pallas_call(
        functools.partial(encoder_body, size, sets, groups[0][1]),
        out_shape=[
            jax.ShapeDtypeStruct(((tile_rows + 4) * wide, 3 * LANES), BF),
            jax.ShapeDtypeStruct((tile_rows // 2, half, 3 * LANES), BF),
        ],
        in_specs=[SMEM, VMEM, VMEM, VMEM] + [HBM] * sets,
        out_specs=[VMEM, VMEM],
        scratch_shapes=[
            packed(weights[0]),
            scratch(3, 3 * tile_rows * wide, 3 * LANES),
            pltpu.VMEM(((tile_rows + 6) * wide, channels), F32),
            pltpu.SemaphoreType.DMA,
        ],
        compiler_params=params(),
        cost_estimate=cost(4 * (2 * tile_rows + 10) * wide),
        name="encoder",
    )(place, cells, lines(enc_first_bias), lines(enc_second_bias), *weights[0])

    tall = tile_rows // 2
    if spread_out:
        others = [lax.ppermute(pooled, "row", cyclic(row_count, by)) for by in range(1, row_count)]
        block1 = laid(block1, after(across(block1, first), pooled))
        far1 = swap_cores(block1)
        next1 = across(block1, second)
        block2 = laid(*here1, cut=(part1, part2))
        block2 = laid(block2, after(across(block2, first), pooled))
        others = after(others, block2)
        part = mid_weight.shape[2]
        bias = lax.dynamic_slice_in_dim(mid_bias, row * part, part, 0)
        rows = tall * row_count
        sent = pl.pallas_call(
            functools.partial(middle_body, size),
            out_shape=[jax.ShapeDtypeStruct((tall + 2, half, 2 * LANES), BF)] * row_count,
            in_specs=[SMEM] + [VMEM] * (row_count + 2),
            out_specs=[VMEM] * row_count,
            scratch_shapes=[
                pltpu.VMEM((rows + 2, half, 3 * LANES), F32),
                scratch(3, (rows + 2) * half, 3 * LANES),
                pltpu.VMEM((rows * half, 2 * LANES), F32),
                scratch(rows + 2, half, 2 * LANES),
            ],
            compiler_params=params(),
            cost_estimate=cost(4 * tile_rows * wide),
            name="middle",
        )(place, pooled, *others, jnp.swapaxes(mid_weight, 1, 2), lines(bias))
        mids = [sent[0]] + [
            lax.ppermute(sent[by], "row", cyclic(row_count, by)) for by in range(1, row_count)
        ]
        next1 = after(next1, sent[0])
        held1 = (block1, next1, far1, swap_cores(next1))
        next2 = after(across(block2, second), *mids)
        held2 = (block2, next2, swap_cores(block2), swap_cores(next2))
        weights += [(own1,) + held1, (own2,) + held2]
    else:
        full = lax.all_gather(mid_weight, "row", axis=2, tiled=True)
        field = jnp.concatenate(
            [lax.ppermute(pooled, "row", down), pooled, lax.ppermute(pooled, "row", [(b, a) for a, b in down])]
        )[:, :, :channels]
        field = jnp.pad(field, ((0, 0), (1, 1), (0, 0)))
        total = jnp.zeros((tall + 2, half, full.shape[2]), F32)
        first = field.shape[0] // 2 - tall // 2 - 2
        for tap in range(9):
            dy, dx = tap // 3, tap % 3
            window = field[first + dy : first + dy + tall + 2, dx : dx + half]
            total += jnp.einsum("rck,kn->rcn", window, full[tap], preferred_element_type=F32)
        at_row = jnp.arange(tall + 2)[:, None, None] - 1 + row * tall
        at_col = jnp.arange(half)[None, :, None] - SIDE // 2 + col * (tile_cols // 2)
        keep = (at_row >= 0) & (at_row < tall * row_count) & (at_col >= 0) & (at_col < tile_cols // 2 * col_count)
        middle = jnp.where(keep, jax.nn.silu(total + mid_bias), 0.0).astype(BF)
        mids = []
        for shard in range(SHARDS):
            block = middle[:, :, 160 * shard : 160 * (shard + 1)]
            tail = jnp.pad(block[:, :, LANES:], ((0, 0), (0, 0), (32 * shard, 96 - 32 * shard)))
            mids.append(jnp.concatenate([block[:, :, :LANES], tail], axis=2))

    field = pl.pallas_call(
        functools.partial(field_body, sets),
        out_shape=jax.ShapeDtypeStruct((5, tall + 2, half, LANES), BF),
        in_specs=[SMEM] + [VMEM] * SHARDS,
        out_specs=VMEM,
        compiler_params=params(),
        cost_estimate=cost(40 * tile_rows * wide),
        name="field",
    )(place, *mids)
    refined = pl.pallas_call(
        functools.partial(joined_body, size, sets, groups[1][1]),
        out_shape=jax.ShapeDtypeStruct(((tile_rows + 2) * wide, 3 * LANES), BF),
        in_specs=[SMEM, VMEM, VMEM, VMEM] + [HBM] * sets,
        out_specs=VMEM,
        scratch_shapes=[
            packed(weights[1]),
            scratch(3, (tile_rows + 4) * wide, 3 * LANES),
            scratch(3, (tile_rows + 4) * wide, 5 * LANES),
            pltpu.VMEM(((tile_rows + 2) * wide, channels), F32),
            pltpu.SemaphoreType.DMA,
        ],
        compiler_params=params(),
        cost_estimate=cost(6 * (tile_rows + 2) * wide),
        name="joined",
    )(place, skip, lines(dec_first_bias), field, *weights[1])
    return pl.pallas_call(
        functools.partial(last_body, size, sets, groups[2][1]),
        out_shape=jax.ShapeDtypeStruct((1, tile_rows, tile_cols, channels), BF),
        in_specs=[SMEM, VMEM, VMEM] + [HBM] * sets,
        out_specs=VMEM,
        scratch_shapes=[
            packed(weights[2]),
            scratch(3, (tile_rows + 2) * wide, 3 * LANES),
            pltpu.VMEM((tile_rows * wide, channels), F32),
            pltpu.SemaphoreType.DMA,
        ],
        compiler_params=params(),
        cost_estimate=cost(2 * tile_rows * wide),
        name="last",
    )(place, refined, lines(dec_second_bias), *weights[2])


def solution(mesh):
    placed = (
        P("grp", "row", "col", None),
        P(None, None, "row"),
        P(),
        P(None, None, "row"),
        P(),
        P(None, None, "row"),
        P(),
        P(None, None, "row"),
        P(),
        P(None, None, "row"),
        P(),
    )
    mesh_shape = tuple(mesh.shape[axis] for axis in AXES)
    return jax.shard_map(
        functools.partial(shards, mesh_shape),
        mesh=mesh,
        in_specs=placed,
        out_specs=P(("grp", "segment"), "row", "col", None),
        check_vma=False,
    )
```

```python
import functools

import jax
import jax.numpy as jnp
from jax import lax
from jax.experimental import pallas as pl
from jax.experimental.pallas import tpu as pltpu
from jax.sharding import PartitionSpec as P

BF = jnp.bfloat16
F32 = jnp.float32
LANES = 128
SIDE = 8
AXES = ("grp", "segment", "row", "col")
PIECES = 8
SHARDS = 4
VMEM = pl.BlockSpec(memory_space=pltpu.VMEM)
HBM = pl.BlockSpec(memory_space=pl.ANY)
SMEM = pl.BlockSpec(memory_space=pltpu.SMEM)


def params():
    return pltpu.CompilerParams(vmem_limit_bytes=52 * 1024 * 1024)


def cost(cells):
    return pl.CostEstimate(flops=cells * 9 * 320 * 640 * 2, bytes_accessed=1 << 20, transcendentals=0)


def plain_chunks(base):
    chunks = [[(tap, base + half * LANES, LANES)] for tap in range(9) for half in range(2)]
    rest = [(tap, base + 256, 64) for tap in range(9)]
    for at in range(0, 9, 2):
        chunks.append(rest[at : at + 2])
    return chunks


def joined_chunks():
    chunks = plain_chunks(0)
    for tap in range(9):
        for shard in range(4):
            chunks.append([(tap, 320 + shard * 160, LANES)])
        chunks.append([(tap, 320 + shard * 160 + LANES, 32) for shard in range(4)])
    return chunks


def padded_count(chunks):
    return -(-len(chunks) // PIECES) * PIECES


def pack_body(layouts, parts, place, *refs):
    count = len(layouts)
    own, mine = refs[count:]
    index = 0
    for chunks, source in zip(layouts, refs):
        channels = source.shape[1]
        for chunk in chunks:
            parts = [source[tap, :, pl.ds(first, size)] for tap, first, size in chunk]
            have = sum(part.shape[1] for part in parts)
            if have < LANES:
                parts.append(jnp.zeros((channels, LANES - have), BF))
            own[index] = parts[0] if len(parts) == 1 else jnp.concatenate(parts, axis=1)
            index += 1
    while index < own.shape[0]:
        own[index] = jnp.zeros(own.shape[1:], BF)
        index += 1
    size = mine.shape[0]
    mine[...] = own[pl.ds(owner_piece(place, parts, place[1], 0) * size, size)]


def pack(layouts, parts, place, weights):
    total = padded_count([chunk for chunks in layouts for chunk in chunks])
    weights = [jnp.swapaxes(weight, 1, 2) for weight in weights]
    channels = weights[0].shape[1]
    return pl.pallas_call(
        functools.partial(pack_body, layouts, parts),
        out_shape=[
            jax.ShapeDtypeStruct((total, channels, LANES), BF),
            jax.ShapeDtypeStruct((total // parts, channels, LANES), BF),
        ],
        in_specs=[SMEM] + [VMEM] * len(weights),
        out_specs=[VMEM, VMEM],
        compiler_params=params(),
        name="pack_weights",
    )(place, *weights)


def piece_body(layouts, parts, place, *refs):
    count = len(layouts)
    sources, mine, held, sems = refs[:count], refs[count], refs[count + 1 : -1], refs[-1]
    copies = [pltpu.make_async_copy(a, b, sems.at[i]) for i, (a, b) in enumerate(zip(sources, held))]
    for copy in copies:
        copy.start()
    for copy in copies:
        copy.wait()
    chunks = [(source, chunk) for source, layer in zip(held, layouts) for chunk in layer]
    size, channels = mine.shape[:2]
    wanted = owner_piece(place, parts, place[1], 0)
    for piece in range(parts):

        @pl.when(wanted == piece)
        def _(piece=piece):
            for index in range(size):
                block = [jnp.zeros((channels, LANES), BF)]
                if piece * size + index < len(chunks):
                    source, chunk = chunks[piece * size + index]
                    block = [source[tap, :, pl.ds(first, width)] for tap, first, width in chunk]
                    have = sum(part.shape[1] for part in block)
                    if have < LANES:
                        block.append(jnp.zeros((channels, LANES - have), BF))
                mine[index] = block[0] if len(block) == 1 else jnp.concatenate(block, axis=1)


def pack_piece(layouts, parts, place, weights):
    total = padded_count([chunk for chunks in layouts for chunk in chunks])
    weights = [jnp.swapaxes(weight, 1, 2) for weight in weights]
    return pl.pallas_call(
        functools.partial(piece_body, layouts, parts),
        out_shape=jax.ShapeDtypeStruct((total // parts, weights[0].shape[1], LANES), BF),
        in_specs=[SMEM] + [HBM] * len(weights),
        out_specs=VMEM,
        scratch_shapes=[pltpu.VMEM(weight.shape, BF) for weight in weights]
        + [pltpu.SemaphoreType.DMA((len(weights),))],
        compiler_params=pltpu.CompilerParams(vmem_limit_bytes=52 * 1024 * 1024),
        name="pack_piece",
    )(place, *weights)


def device_pairs(mesh_shape, move):
    grps, segs, rows, cols = mesh_shape
    place = lambda g, s, r, c: ((g * segs + s) * rows + r) * cols + c
    return [
        (place(g, s, r, c), place(*move(g, s, r, c)))
        for g in range(grps)
        for s in range(segs)
        for r in range(rows)
        for c in range(cols)
    ]


def cyclic(count, by):
    return [(i, (i + by) % count) for i in range(count)]


def after(value, *others):
    return lax.optimization_barrier((value,) + others)[0]


def laid_body(cuts, *refs):
    count = len(cuts)
    sources, target, sems = refs[:count], refs[count], refs[count + 1]
    copies, at = [], 0
    for index, (source, (first, size)) in enumerate(zip(sources, cuts)):
        copies.append(
            pltpu.make_async_copy(
                source.at[pl.ds(first, size)], target.at[pl.ds(at, size)], sems.at[index]
            )
        )
        at += size
    for copy in copies:
        copy.start()
    for copy in copies:
        copy.wait()


def laid(*parts, cut=None):
    cuts = tuple(cut or (0, part.shape[0]) for part in parts)
    return pl.pallas_call(
        functools.partial(laid_body, cuts),
        out_shape=jax.ShapeDtypeStruct((sum(size for _, size in cuts),) + parts[0].shape[1:], BF),
        in_specs=[HBM] * len(parts),
        out_specs=VMEM,
        scratch_shapes=[pltpu.SemaphoreType.DMA((len(parts),))],
        compiler_params=params(),
        cost_estimate=pl.CostEstimate(flops=0, bytes_accessed=1 << 21, transcendentals=0),
        name="laid",
    )(*parts)


def from_planes(mine, count):
    return [lax.ppermute(mine, "row", cyclic(count, by)) for by in range(1, count)]


def plane_moves(mesh_shape):
    first = device_pairs(
        mesh_shape, lambda g, s, r, c: (g, s, r, 1 - c) if s == 0 else (1 - g, s, r, c)
    )
    second = device_pairs(
        mesh_shape, lambda g, s, r, c: (1 - g, s, r, c) if s == 0 else (g, s, r, 1 - c)
    )
    return first, second


def swap_cores(block):
    return lax.ppermute(block, "segment", [(0, 1), (1, 0)])


def owner_piece(place, parts, core, slot):
    grp, col = place[0], place[3]
    low, high = slot % 2, slot // 2
    if parts == 4:
        col, grp = (1 - col, 1 - grp) if low else (col, grp)
        return jnp.where(core == 0, col, 2 + grp)
    flip_col = jnp.where(core == 0, low, high)
    flip_grp = jnp.where(core == 0, high, low)
    grp = jnp.where(flip_grp == 1, 1 - grp, grp)
    col = jnp.where(flip_col == 1, 1 - col, col)
    return (grp * 2 + core) * 2 + col


def load_weights(place, parts, sources, target, sem):
    if len(sources) == 1:
        return [pltpu.make_async_copy(sources[0], target, sem)]
    own, near0, near1, far0, far1 = sources
    seg, row = place[1], place[2]
    size = own.shape[0] // parts
    each = parts // 4
    copies = [pltpu.make_async_copy(own, target.at[:, row], sem)]
    for pair, core in (((near0, near1), seg), ((far0, far1), 1 - seg)):
        for slot in range(2 * each):
            array = pair[slot // each]
            piece = owner_piece(place, parts, core, slot)
            for by in range(1, SHARDS):
                shard = lax.rem(row - by + SHARDS, SHARDS)
                source = array.at[pl.ds(((slot % each) * 3 + by - 1) * size, size)]
                copies.append(
                    pltpu.make_async_copy(source, target.at[pl.ds(piece * size, size), shard], sem)
                )
    return copies


def silu(value):
    return value / (1.0 + jnp.exp(-value))


def spread(value, shifted):
    cells = value.shape[0]
    shifted[0, :cells] = pltpu.roll(value, 1, 0).astype(BF)
    shifted[1, :cells] = value.astype(BF)
    shifted[2, :cells] = pltpu.roll(value, cells - 1, 0).astype(BF)


def weight_pair(weights, low, high):
    parts = []
    for index in (low, high):
        if index is not None:
            block = weights[index]
            parts.append(block.reshape(block.shape[0] * block.shape[1], LANES))
    return parts[0] if len(parts) == 1 else jnp.concatenate(parts, axis=1)


def product(left, right):
    return lax.dot_general(left, right, (((1,), (1,)), ((), ())), preferred_element_type=F32)


def add_plain(shifted, weights, base, rows, wide, acc, bias):
    cells = rows * wide

    def window(tap, first, size):
        at = (tap // 3) * wide
        return shifted[tap % 3, pl.ds(at, cells), pl.ds(first, size)]

    def rest(at):
        low = window(2 * at, 256, LANES)
        if at == 4:
            return low
        high = window(2 * at + 1, 256, LANES)
        lane = lax.broadcasted_iota(jnp.int32, (cells, LANES), 1)
        return jnp.where(lane < 64, low, high)

    acc[:cells] = product(window(0, 0, 256), weight_pair(weights, base, base + 1)) + bias
    for tap in range(1, 9):
        acc[:cells] += product(window(tap, 0, 256), weight_pair(weights, base + 2 * tap, base + 2 * tap + 1))
    for at in range(0, 4, 2):
        left = jnp.concatenate([rest(at), rest(at + 1)], axis=1)
        acc[:cells] += product(left, weight_pair(weights, base + 18 + at, base + 19 + at))
    acc[:cells] += product(rest(4), weight_pair(weights, base + 22, None))


def inside(place, rows, wide, first_row, first_col, size):
    tile_rows, tile_cols, row_count, col_count = size
    row = lax.broadcasted_iota(jnp.int32, (rows, wide, 1), 0) + (place[2] * tile_rows + first_row)
    col = lax.broadcasted_iota(jnp.int32, (rows, wide, 1), 1) + (place[3] * tile_cols + first_col)
    return (row >= 0) & (row < tile_rows * row_count) & (col >= 0) & (col < tile_cols * col_count)


def activated(acc, rows, wide, keep):
    value = silu(acc[: rows * wide]).reshape(rows, wide, acc.shape[1])
    value = jnp.where(keep, value, 0.0).reshape(rows * wide, acc.shape[1])
    value = value.astype(BF).astype(F32)
    return jnp.concatenate([value, value[:, 256:320]], axis=1)


def encoder_body(size, sets, parts, place, cells, bias1, bias2, *refs):
    tile_rows, tile_cols = size[:2]
    wide = tile_cols + 2 * SIDE
    sources, refs = refs[:sets], refs[sets:]
    skip, pooled, weights, shifted, acc, sem = refs
    copies = load_weights(place, parts, sources, weights, sem)
    for copy in copies:
        copy.start()
    spread(cells[...].astype(F32), shifted)
    for copy in copies:
        copy.wait()
    rows = tile_rows + 6
    add_plain(shifted, weights, 0, rows, wide, acc, bias1[...])
    hidden = activated(acc, rows, wide, inside(place, rows, wide, -3, -SIDE, size))
    spread(hidden, shifted)
    rows = tile_rows + 4
    add_plain(shifted, weights, 23, rows, wide, acc, bias2[...])
    value = activated(acc, rows, wide, inside(place, rows, wide, -2, -SIDE, size)).astype(BF)
    skip[...] = value
    half = pooled.shape[1]
    cell = lax.broadcasted_iota(jnp.int32, (half, 2 * wide), 1)
    cell = jnp.where(cell >= wide, cell - wide, cell)
    target = lax.broadcasted_iota(jnp.int32, (half, 2 * wide), 0)
    mean = jnp.where(cell // 2 == target, 0.25, 0.0).astype(BF)
    for row in range(tile_rows // 2):
        at = (2 + 2 * row) * wide
        block = value[at : at + 2 * wide]
        pooled[row] = jnp.dot(mean, block, preferred_element_type=F32).astype(BF)


def middle_body(size, place, own, *refs):
    tile_rows, tile_cols, row_count, col_count = size
    others, refs = refs[: row_count - 1], refs[row_count - 1 :]
    weights, bias = refs[:2]
    outs, refs = refs[2 : 2 + row_count], refs[2 + row_count :]
    field, shifted, acc, result = refs
    row = place[2]
    tall, half = tile_rows // 2, own.shape[1]
    rows = tall * row_count
    flat = (rows + 2) * half
    field[0] = jnp.zeros_like(field[0])
    field[rows + 1] = jnp.zeros_like(field[0])
    for by in range(row_count):
        source = own if by == 0 else others[by - 1]
        at = lax.rem(row - by + row_count, row_count)
        field[pl.ds(1 + tall * at, tall)] = source[...].astype(F32)
    spread(field[...].reshape(flat, field.shape[2]), shifted)
    cells = rows * half
    channels = weights.shape[1]
    acc[...] = jnp.zeros_like(acc)
    for tap in range(9):
        at = (tap // 3) * half
        left = shifted[tap % 3, pl.ds(at, cells), :]
        part = product(left[:, :256], weights[tap, :, :256])
        part += product(left[:, 256:320], weights[tap, :, 256:320])
        if tap == 0:
            part += bias[...]
        acc[:, :channels] += part
    col = lax.broadcasted_iota(jnp.int32, (rows, half, 1), 1)
    col = col + (place[3] * (tile_cols // 2) - SIDE // 2)
    keep = (col >= 0) & (col < tile_cols // 2 * col_count)
    value = silu(acc[...]).reshape(rows, half, 2 * LANES)
    value = jnp.where(keep, value, 0.0).reshape(cells, 2 * LANES)
    tail = pltpu.roll(value[:, LANES:], row * 32, 1)
    value = jnp.concatenate([value[:, :LANES], tail], axis=1).astype(BF)
    result[0] = jnp.zeros_like(result[0])
    result[rows + 1] = jnp.zeros_like(result[0])
    result[1 : rows + 1] = value.reshape(rows, half, 2 * LANES)
    for by in range(row_count):
        at = lax.rem(row + by, row_count)
        outs[by][...] = result[pl.ds(tall * at, tall + 2)]


def field_body(sets, place, *refs):
    mids, field = refs[:SHARDS], refs[SHARDS]
    tail = mids[0][:, :, LANES:]
    for mid in mids[1:]:
        tail = tail + mid[:, :, LANES:]
    field[4] = tail
    for by in range(SHARDS):
        shard = lax.rem(place[2] - by + SHARDS, SHARDS) if sets > 1 else by
        field[shard] = mids[by][:, :, :LANES]


def joined_body(size, sets, parts, place, skip, bias, *refs):
    tile_rows, tile_cols = size[:2]
    wide = tile_cols + 2 * SIDE
    field, refs = refs[0], refs[1:]
    sources, refs = refs[:sets], refs[sets:]
    out, weights, shifted, raised, acc, sem = refs
    copies = load_weights(place, parts, sources, weights, sem)
    for copy in copies:
        copy.start()
    spread(skip[...].astype(F32), shifted)
    half = field.shape[2]
    tall = tile_rows // 2 + 2
    cell = lax.broadcasted_iota(jnp.int32, (3 * wide, half), 0)
    move = jnp.where(cell >= 2 * wide, 1 - 2 * wide, jnp.where(cell >= wide, -wide, -1))
    source = lax.broadcasted_iota(jnp.int32, (3 * wide, half), 1)
    place_of = cell + move
    raise_by = jnp.where((place_of >= 2 * source) & (place_of < 2 * source + 2), 1.0, 0.0).astype(BF)
    for row in range(tall):
        block = jnp.concatenate([field[chunk, row] for chunk in range(5)], axis=1)
        up = jnp.dot(raise_by, block, preferred_element_type=F32).astype(BF)
        for dx in range(3):
            for twice in range(2):
                at = (2 * row + twice) * wide
                raised[dx, at : at + wide] = up[dx * wide : (dx + 1) * wide]
    for copy in copies:
        copy.wait()
    rows = tile_rows + 2
    cells = rows * wide
    add_plain(shifted, weights, 0, rows, wide, acc, bias[...])

    def window(tap, first, count):
        return raised[tap % 3, pl.ds((tap // 3) * wide, cells), pl.ds(first, count)]

    for tap in range(9):
        at = 23 + 5 * tap
        for pair in range(2):
            left = window(tap, 256 * pair, 256)
            acc[:cells] += product(left, weight_pair(weights, at + 2 * pair, at + 2 * pair + 1))
        if tap % 2 == 1:
            left = jnp.concatenate([window(tap - 1, 512, LANES), window(tap, 512, LANES)], axis=1)
            acc[:cells] += product(left, weight_pair(weights, at - 1, at + 4))
        elif tap == 8:
            acc[:cells] += product(window(tap, 512, LANES), weight_pair(weights, at + 4, None))
    out[...] = activated(acc, rows, wide, inside(place, rows, wide, -1, -SIDE, size)).astype(BF)


def last_body(size, sets, parts, place, refined, bias, *refs):
    tile_rows, tile_cols = size[:2]
    wide = tile_cols + 2 * SIDE
    sources, refs = refs[:sets], refs[sets:]
    out, weights, shifted, acc, sem = refs
    copies = load_weights(place, parts, sources, weights, sem)
    for copy in copies:
        copy.start()
    spread(refined[...].astype(F32), shifted)
    for copy in copies:
        copy.wait()
    add_plain(shifted, weights, 0, tile_rows, wide, acc, bias[...])
    value = silu(acc[...]).reshape(tile_rows, wide, acc.shape[1])
    out[0] = value[:, SIDE : SIDE + tile_cols, :].astype(BF)


def shards(mesh_shape, latent, enc_first, enc_first_bias, enc_second, enc_second_bias, mid_weight, mid_bias,
           dec_first, dec_first_bias, dec_second, dec_second_bias):
    grps, segs, row_count, col_count = mesh_shape
    grp, seg, row, col = (lax.axis_index(axis) for axis in AXES)
    place = jnp.stack([grp, seg, row, col]).astype(jnp.int32)
    tile_rows, tile_cols, channels = latent.shape[1:]
    size = (tile_rows, tile_cols, row_count, col_count)
    wide = tile_cols + 2 * SIDE
    half = -(-(wide // 2) // 16) * 16
    spread_out = row_count == SHARDS and col_count == 2 and grps == 2 and segs == 2
    plain, joined = plain_chunks(0), joined_chunks()

    groups = (
        ((plain, plain), 8, (enc_first, enc_second)),
        ((joined,), 8, (dec_first,)),
        ((plain,), 8, (dec_second,)),
    )
    if spread_out:
        mine0 = pack_piece(groups[0][0], groups[0][1], place, groups[0][2])
        later = after(place, mine0)
        (own0, _), (own1, mine1), (own2, mine2) = (
            pack(layouts, parts, later, group) for layouts, parts, group in groups
        )

    tile = lax.dynamic_index_in_dim(latent, seg, 0, keepdims=False)
    if spread_out:
        tile = after(tile, mine0)
    down = [(i, i + 1) for i in range(row_count - 1)]
    above = lax.ppermute(tile, "row", down)
    below = lax.ppermute(tile, "row", [(b, a) for a, b in down])
    tile = jnp.concatenate([above, tile, below], axis=0)
    left_edge, right_edge = tile[:, :SIDE], tile[:, tile_cols - SIDE :]
    if col_count == 2:
        edge = lax.ppermute(jnp.where(col == 0, right_edge, left_edge), "col", [(0, 1), (1, 0)])
        blank = jnp.zeros_like(edge)
        left, right = jnp.where(col == 0, blank, edge), jnp.where(col == 0, edge, blank)
    else:
        along = [(i, i + 1) for i in range(col_count - 1)]
        left = lax.ppermute(right_edge, "col", along)
        right = lax.ppermute(left_edge, "col", [(b, a) for a, b in along])
        edge = left
    tile = jnp.concatenate([left, tile, right], axis=1)
    cells = jnp.concatenate([tile, tile[:, :, 256:]], axis=2).reshape(-1, 3 * LANES)

    sets = 5 if spread_out else 1
    weights = []
    if spread_out:
        first, second = plane_moves(mesh_shape)
        across = lambda block, pairs: lax.ppermute(block, AXES, pairs)
        here0 = from_planes(mine0, row_count)
        late = laid(mine1, mine2)
        here1 = from_planes(late, row_count)
        block0 = laid(*after(here0, late, own0))
        block0 = laid(block0, across(block0, first))
        block0 = after(block0, here1[0], above, below)
        far0 = swap_cores(block0)
        next0 = after(across(block0, second), edge, here1[1], here1[2])
        held0 = (block0, next0, far0, swap_cores(next0))
        part1, part2 = mine1.shape[0], mine2.shape[0]
        block1 = laid(*here1, cut=(0, part1))
        weights = [(own0,) + held0]
    else:
        for layouts, parts, group in groups:
            full = [lax.all_gather(weight, "row", axis=2, tiled=True) for weight in group]
            own = pack(layouts, parts, place, full)[0]
            weights.append((own.reshape(own.shape[0], SHARDS, -1, LANES),))

    scratch = lambda *shape: pltpu.VMEM(shape, BF)
    lines = lambda bias: bias.reshape(1, -1)
    packed = lambda source: scratch(source[0].shape[0], SHARDS, channels // SHARDS, LANES)
    skip, pooled = pl.pallas_call(
        functools.partial(encoder_body, size, sets, groups[0][1]),
        out_shape=[
            jax.ShapeDtypeStruct(((tile_rows + 4) * wide, 3 * LANES), BF),
            jax.ShapeDtypeStruct((tile_rows // 2, half, 3 * LANES), BF),
        ],
        in_specs=[SMEM, VMEM, VMEM, VMEM] + [HBM] * sets,
        out_specs=[VMEM, VMEM],
        scratch_shapes=[
            packed(weights[0]),
            scratch(3, 3 * tile_rows * wide, 3 * LANES),
            pltpu.VMEM(((tile_rows + 6) * wide, channels), F32),
            pltpu.SemaphoreType.DMA,
        ],
        compiler_params=params(),
        cost_estimate=cost(4 * (2 * tile_rows + 10) * wide),
        name="encoder",
    )(place, cells, lines(enc_first_bias), lines(enc_second_bias), *weights[0])

    tall = tile_rows // 2
    if spread_out:
        others = [lax.ppermute(pooled, "row", cyclic(row_count, by)) for by in range(1, row_count)]
        block1 = laid(block1, after(across(block1, first), pooled))
        far1 = swap_cores(block1)
        next1 = across(block1, second)
        block2 = laid(*here1, cut=(part1, part2))
        block2 = laid(block2, after(across(block2, first), pooled))
        others = after(others, block2)
        part = mid_weight.shape[2]
        bias = lax.dynamic_slice_in_dim(mid_bias, row * part, part, 0)
        rows = tall * row_count
        sent = pl.pallas_call(
            functools.partial(middle_body, size),
            out_shape=[jax.ShapeDtypeStruct((tall + 2, half, 2 * LANES), BF)] * row_count,
            in_specs=[SMEM] + [VMEM] * (row_count + 2),
            out_specs=[VMEM] * row_count,
            scratch_shapes=[
                pltpu.VMEM((rows + 2, half, 3 * LANES), F32),
                scratch(3, (rows + 2) * half, 3 * LANES),
                pltpu.VMEM((rows * half, 2 * LANES), F32),
                scratch(rows + 2, half, 2 * LANES),
            ],
            compiler_params=params(),
            cost_estimate=cost(4 * tile_rows * wide),
            name="middle",
        )(place, pooled, *others, jnp.swapaxes(mid_weight, 1, 2), lines(bias))
        mids = [sent[0]] + [
            lax.ppermute(sent[by], "row", cyclic(row_count, by)) for by in range(1, row_count)
        ]
        next1 = after(next1, sent[0])
        held1 = (block1, next1, far1, swap_cores(next1))
        next2 = after(across(block2, second), *mids)
        held2 = (block2, next2, swap_cores(block2), swap_cores(next2))
        weights += [(own1,) + held1, (own2,) + held2]
    else:
        full = lax.all_gather(mid_weight, "row", axis=2, tiled=True)
        field = jnp.concatenate(
            [lax.ppermute(pooled, "row", down), pooled, lax.ppermute(pooled, "row", [(b, a) for a, b in down])]
        )[:, :, :channels]
        field = jnp.pad(field, ((0, 0), (1, 1), (0, 0)))
        total = jnp.zeros((tall + 2, half, full.shape[2]), F32)
        first = field.shape[0] // 2 - tall // 2 - 2
        for tap in range(9):
            dy, dx = tap // 3, tap % 3
            window = field[first + dy : first + dy + tall + 2, dx : dx + half]
            total += jnp.einsum("rck,kn->rcn", window, full[tap], preferred_element_type=F32)
        at_row = jnp.arange(tall + 2)[:, None, None] - 1 + row * tall
        at_col = jnp.arange(half)[None, :, None] - SIDE // 2 + col * (tile_cols // 2)
        keep = (at_row >= 0) & (at_row < tall * row_count) & (at_col >= 0) & (at_col < tile_cols // 2 * col_count)
        middle = jnp.where(keep, jax.nn.silu(total + mid_bias), 0.0).astype(BF)
        mids = []
        for shard in range(SHARDS):
            block = middle[:, :, 160 * shard : 160 * (shard + 1)]
            tail = jnp.pad(block[:, :, LANES:], ((0, 0), (0, 0), (32 * shard, 96 - 32 * shard)))
            mids.append(jnp.concatenate([block[:, :, :LANES], tail], axis=2))

    field = pl.pallas_call(
        functools.partial(field_body, sets),
        out_shape=jax.ShapeDtypeStruct((5, tall + 2, half, LANES), BF),
        in_specs=[SMEM] + [VMEM] * SHARDS,
        out_specs=VMEM,
        compiler_params=params(),
        cost_estimate=cost(40 * tile_rows * wide),
        name="field",
    )(place, *mids)
    refined = pl.pallas_call(
        functools.partial(joined_body, size, sets, groups[1][1]),
        out_shape=jax.ShapeDtypeStruct(((tile_rows + 2) * wide, 3 * LANES), BF),
        in_specs=[SMEM, VMEM, VMEM, VMEM] + [HBM] * sets,
        out_specs=VMEM,
        scratch_shapes=[
            packed(weights[1]),
            scratch(3, (tile_rows + 4) * wide, 3 * LANES),
            scratch(3, (tile_rows + 4) * wide, 5 * LANES),
            pltpu.VMEM(((tile_rows + 2) * wide, channels), F32),
            pltpu.SemaphoreType.DMA,
        ],
        compiler_params=params(),
        cost_estimate=cost(6 * (tile_rows + 2) * wide),
        name="joined",
    )(place, skip, lines(dec_first_bias), field, *weights[1])
    return pl.pallas_call(
        functools.partial(last_body, size, sets, groups[2][1]),
        out_shape=jax.ShapeDtypeStruct((1, tile_rows, tile_cols, channels), BF),
        in_specs=[SMEM, VMEM, VMEM] + [HBM] * sets,
        out_specs=VMEM,
        scratch_shapes=[
            packed(weights[2]),
            scratch(3, (tile_rows + 2) * wide, 3 * LANES),
            pltpu.VMEM((tile_rows * wide, channels), F32),
            pltpu.SemaphoreType.DMA,
        ],
        compiler_params=params(),
        cost_estimate=cost(2 * tile_rows * wide),
        name="last",
    )(place, refined, lines(dec_second_bias), *weights[2])


def solution(mesh):
    placed = (
        P("grp", "row", "col", None),
        P(None, None, "row"),
        P(),
        P(None, None, "row"),
        P(),
        P(None, None, "row"),
        P(),
        P(None, None, "row"),
        P(),
        P(None, None, "row"),
        P(),
    )
    mesh_shape = tuple(mesh.shape[axis] for axis in AXES)
    return jax.shard_map(
        functools.partial(shards, mesh_shape),
        mesh=mesh,
        in_specs=placed,
        out_specs=P(("grp", "segment"), "row", "col", None),
        check_vma=False,
    )
```

```python
import functools

import jax
import jax.numpy as jnp
from jax import lax
from jax.experimental import pallas as pl
from jax.experimental.pallas import tpu as pltpu
from jax.sharding import PartitionSpec as P

BF = jnp.bfloat16
F32 = jnp.float32
LANES = 128
SIDE = 8
AXES = ("grp", "segment", "row", "col")
PIECES = 8
SHARDS = 4
VMEM = pl.BlockSpec(memory_space=pltpu.VMEM)
HBM = pl.BlockSpec(memory_space=pl.ANY)
SMEM = pl.BlockSpec(memory_space=pltpu.SMEM)


def params():
    return pltpu.CompilerParams(vmem_limit_bytes=36 * 1024 * 1024)


def cost(cells):
    return pl.CostEstimate(flops=cells * 9 * 320 * 640 * 2, bytes_accessed=1 << 20, transcendentals=0)


def plain_chunks(base):
    chunks = [[(tap, base + half * LANES, LANES)] for tap in range(9) for half in range(2)]
    rest = [(tap, base + 256, 64) for tap in range(9)]
    for at in range(0, 9, 2):
        chunks.append(rest[at : at + 2])
    return chunks


def joined_chunks():
    chunks = plain_chunks(0)
    for tap in range(9):
        for shard in range(4):
            chunks.append([(tap, 320 + shard * 160, LANES)])
        chunks.append([(tap, 320 + shard * 160 + LANES, 32) for shard in range(4)])
    return chunks


def padded_count(chunks):
    return -(-len(chunks) // PIECES) * PIECES


def pack_body(layouts, parts, place, *refs):
    count = len(layouts)
    own, mine = refs[count:]
    index = 0
    for chunks, source in zip(layouts, refs):
        channels = source.shape[1]
        for chunk in chunks:
            parts = [source[tap, :, pl.ds(first, size)] for tap, first, size in chunk]
            have = sum(part.shape[1] for part in parts)
            if have < LANES:
                parts.append(jnp.zeros((channels, LANES - have), BF))
            own[index] = parts[0] if len(parts) == 1 else jnp.concatenate(parts, axis=1)
            index += 1
    while index < own.shape[0]:
        own[index] = jnp.zeros(own.shape[1:], BF)
        index += 1
    size = mine.shape[0]
    mine[...] = own[pl.ds(owner_piece(place, parts, place[1], 0) * size, size)]


def pack(layouts, parts, place, weights):
    total = padded_count([chunk for chunks in layouts for chunk in chunks])
    weights = [jnp.swapaxes(weight, 1, 2) for weight in weights]
    channels = weights[0].shape[1]
    return pl.pallas_call(
        functools.partial(pack_body, layouts, parts),
        out_shape=[
            jax.ShapeDtypeStruct((total, channels, LANES), BF),
            jax.ShapeDtypeStruct((total // parts, channels, LANES), BF),
        ],
        in_specs=[SMEM] + [VMEM] * len(weights),
        out_specs=[VMEM, VMEM],
        compiler_params=params(),
        name="pack_weights",
    )(place, *weights)


def piece_body(layouts, parts, place, *refs):
    count = len(layouts)
    sources, mine, held, sems = refs[:count], refs[count], refs[count + 1 : -1], refs[-1]
    copies = [pltpu.make_async_copy(a, b, sems.at[i]) for i, (a, b) in enumerate(zip(sources, held))]
    for copy in copies:
        copy.start()
    for copy in copies:
        copy.wait()
    chunks = [(source, chunk) for source, layer in zip(held, layouts) for chunk in layer]
    size, channels = mine.shape[:2]
    wanted = owner_piece(place, parts, place[1], 0)
    for piece in range(parts):

        @pl.when(wanted == piece)
        def _(piece=piece):
            for index in range(size):
                block = [jnp.zeros((channels, LANES), BF)]
                if piece * size + index < len(chunks):
                    source, chunk = chunks[piece * size + index]
                    block = [source[tap, :, pl.ds(first, width)] for tap, first, width in chunk]
                    have = sum(part.shape[1] for part in block)
                    if have < LANES:
                        block.append(jnp.zeros((channels, LANES - have), BF))
                mine[index] = block[0] if len(block) == 1 else jnp.concatenate(block, axis=1)


def pack_piece(layouts, parts, place, weights):
    total = padded_count([chunk for chunks in layouts for chunk in chunks])
    weights = [jnp.swapaxes(weight, 1, 2) for weight in weights]
    return pl.pallas_call(
        functools.partial(piece_body, layouts, parts),
        out_shape=jax.ShapeDtypeStruct((total // parts, weights[0].shape[1], LANES), BF),
        in_specs=[SMEM] + [HBM] * len(weights),
        out_specs=VMEM,
        scratch_shapes=[pltpu.VMEM(weight.shape, BF) for weight in weights]
        + [pltpu.SemaphoreType.DMA((len(weights),))],
        compiler_params=pltpu.CompilerParams(vmem_limit_bytes=52 * 1024 * 1024),
        name="pack_piece",
    )(place, *weights)


def device_pairs(mesh_shape, move):
    grps, segs, rows, cols = mesh_shape
    place = lambda g, s, r, c: ((g * segs + s) * rows + r) * cols + c
    return [
        (place(g, s, r, c), place(*move(g, s, r, c)))
        for g in range(grps)
        for s in range(segs)
        for r in range(rows)
        for c in range(cols)
    ]


def cyclic(count, by):
    return [(i, (i + by) % count) for i in range(count)]


def after(value, *others):
    return lax.optimization_barrier((value,) + others)[0]


def laid_body(cuts, *refs):
    count = len(cuts)
    sources, target, sems = refs[:count], refs[count], refs[count + 1]
    copies, at = [], 0
    for index, (source, (first, size)) in enumerate(zip(sources, cuts)):
        copies.append(
            pltpu.make_async_copy(
                source.at[pl.ds(first, size)], target.at[pl.ds(at, size)], sems.at[index]
            )
        )
        at += size
    for copy in copies:
        copy.start()
    for copy in copies:
        copy.wait()


def laid(*parts, cut=None):
    cuts = tuple(cut or (0, part.shape[0]) for part in parts)
    return pl.pallas_call(
        functools.partial(laid_body, cuts),
        out_shape=jax.ShapeDtypeStruct((sum(size for _, size in cuts),) + parts[0].shape[1:], BF),
        in_specs=[HBM] * len(parts),
        out_specs=VMEM,
        scratch_shapes=[pltpu.SemaphoreType.DMA((len(parts),))],
        compiler_params=params(),
        cost_estimate=pl.CostEstimate(flops=0, bytes_accessed=1 << 21, transcendentals=0),
        name="laid",
    )(*parts)


def from_planes(mine, count):
    return [lax.ppermute(mine, "row", cyclic(count, by)) for by in range(1, count)]


def plane_moves(mesh_shape):
    first = device_pairs(
        mesh_shape, lambda g, s, r, c: (g, s, r, 1 - c) if s == 0 else (1 - g, s, r, c)
    )
    second = device_pairs(
        mesh_shape, lambda g, s, r, c: (1 - g, s, r, c) if s == 0 else (g, s, r, 1 - c)
    )
    return first, second


def swap_cores(block):
    return lax.ppermute(block, "segment", [(0, 1), (1, 0)])


def owner_piece(place, parts, core, slot):
    grp, col = place[0], place[3]
    low, high = slot % 2, slot // 2
    if parts == 4:
        col, grp = (1 - col, 1 - grp) if low else (col, grp)
        return jnp.where(core == 0, col, 2 + grp)
    flip_col = jnp.where(core == 0, low, high)
    flip_grp = jnp.where(core == 0, high, low)
    grp = jnp.where(flip_grp == 1, 1 - grp, grp)
    col = jnp.where(flip_col == 1, 1 - col, col)
    return (grp * 2 + core) * 2 + col


def load_weights(place, parts, sources, target, sem):
    if len(sources) == 1:
        return [pltpu.make_async_copy(sources[0], target, sem)]
    own, near0, near1, far0, far1 = sources
    seg, row = place[1], place[2]
    size = own.shape[0] // parts
    each = parts // 4
    copies = [pltpu.make_async_copy(own, target.at[:, row], sem)]
    for pair, core in (((near0, near1), seg), ((far0, far1), 1 - seg)):
        for slot in range(2 * each):
            array = pair[slot // each]
            piece = owner_piece(place, parts, core, slot)
            for by in range(1, SHARDS):
                shard = lax.rem(row - by + SHARDS, SHARDS)
                source = array.at[pl.ds(((slot % each) * 3 + by - 1) * size, size)]
                copies.append(
                    pltpu.make_async_copy(source, target.at[pl.ds(piece * size, size), shard], sem)
                )
    return copies


def silu(value):
    return value / (1.0 + jnp.exp(-value))


def spread(value, shifted):
    cells = value.shape[0]
    shifted[0, :cells] = pltpu.roll(value, 1, 0).astype(BF)
    shifted[1, :cells] = value.astype(BF)
    shifted[2, :cells] = pltpu.roll(value, cells - 1, 0).astype(BF)


def weight_pair(weights, low, high):
    parts = []
    for index in (low, high):
        if index is not None:
            block = weights[index]
            parts.append(block.reshape(block.shape[0] * block.shape[1], LANES))
    return parts[0] if len(parts) == 1 else jnp.concatenate(parts, axis=1)


def product(left, right):
    return lax.dot_general(left, right, (((1,), (1,)), ((), ())), preferred_element_type=F32)


def add_plain(shifted, weights, base, rows, wide, acc, bias):
    cells = rows * wide

    def window(tap, first, size):
        at = (tap // 3) * wide
        return shifted[tap % 3, pl.ds(at, cells), pl.ds(first, size)]

    def rest(at):
        low = window(2 * at, 256, LANES)
        if at == 4:
            return low
        high = window(2 * at + 1, 256, LANES)
        lane = lax.broadcasted_iota(jnp.int32, (cells, LANES), 1)
        return jnp.where(lane < 64, low, high)

    acc[:cells] = product(window(0, 0, 256), weight_pair(weights, base, base + 1)) + bias
    for tap in range(1, 9):
        acc[:cells] += product(window(tap, 0, 256), weight_pair(weights, base + 2 * tap, base + 2 * tap + 1))
    for at in range(0, 4, 2):
        left = jnp.concatenate([rest(at), rest(at + 1)], axis=1)
        acc[:cells] += product(left, weight_pair(weights, base + 18 + at, base + 19 + at))
    acc[:cells] += product(rest(4), weight_pair(weights, base + 22, None))


def inside(place, rows, wide, first_row, first_col, size):
    tile_rows, tile_cols, row_count, col_count = size
    row = lax.broadcasted_iota(jnp.int32, (rows, wide, 1), 0) + (place[2] * tile_rows + first_row)
    col = lax.broadcasted_iota(jnp.int32, (rows, wide, 1), 1) + (place[3] * tile_cols + first_col)
    return (row >= 0) & (row < tile_rows * row_count) & (col >= 0) & (col < tile_cols * col_count)


def activated(acc, rows, wide, keep):
    value = silu(acc[: rows * wide]).reshape(rows, wide, acc.shape[1])
    value = jnp.where(keep, value, 0.0).reshape(rows * wide, acc.shape[1])
    value = value.astype(BF).astype(F32)
    return jnp.concatenate([value, value[:, 256:320]], axis=1)


def encoder_body(size, sets, parts, place, cells, bias1, bias2, *refs):
    tile_rows, tile_cols = size[:2]
    wide = tile_cols + 2 * SIDE
    sources, refs = refs[:sets], refs[sets:]
    skip, pooled, weights, shifted, acc, sem = refs
    copies = load_weights(place, parts, sources, weights, sem)
    for copy in copies:
        copy.start()
    spread(cells[...].astype(F32), shifted)
    for copy in copies:
        copy.wait()
    rows = tile_rows + 6
    add_plain(shifted, weights, 0, rows, wide, acc, bias1[...])
    hidden = activated(acc, rows, wide, inside(place, rows, wide, -3, -SIDE, size))
    spread(hidden, shifted)
    rows = tile_rows + 4
    add_plain(shifted, weights, 23, rows, wide, acc, bias2[...])
    value = activated(acc, rows, wide, inside(place, rows, wide, -2, -SIDE, size)).astype(BF)
    skip[...] = value
    half = pooled.shape[1]
    cell = lax.broadcasted_iota(jnp.int32, (half, 2 * wide), 1)
    cell = jnp.where(cell >= wide, cell - wide, cell)
    target = lax.broadcasted_iota(jnp.int32, (half, 2 * wide), 0)
    mean = jnp.where(cell // 2 == target, 0.25, 0.0).astype(BF)
    for row in range(tile_rows // 2):
        at = (2 + 2 * row) * wide
        block = value[at : at + 2 * wide]
        pooled[row] = jnp.dot(mean, block, preferred_element_type=F32).astype(BF)


def middle_body(size, place, own, *refs):
    tile_rows, tile_cols, row_count, col_count = size
    others, refs = refs[: row_count - 1], refs[row_count - 1 :]
    weights, bias = refs[:2]
    outs, refs = refs[2 : 2 + row_count], refs[2 + row_count :]
    field, shifted, acc, result = refs
    row = place[2]
    tall, half = tile_rows // 2, own.shape[1]
    rows = tall * row_count
    flat = (rows + 2) * half
    field[0] = jnp.zeros_like(field[0])
    field[rows + 1] = jnp.zeros_like(field[0])
    for by in range(row_count):
        source = own if by == 0 else others[by - 1]
        at = lax.rem(row - by + row_count, row_count)
        field[pl.ds(1 + tall * at, tall)] = source[...].astype(F32)
    spread(field[...].reshape(flat, field.shape[2]), shifted)
    cells = rows * half
    channels = weights.shape[1]
    acc[...] = jnp.zeros_like(acc)
    for tap in range(9):
        at = (tap // 3) * half
        left = shifted[tap % 3, pl.ds(at, cells), :]
        part = product(left[:, :256], weights[tap, :, :256])
        part += product(left[:, 256:320], weights[tap, :, 256:320])
        if tap == 0:
            part += bias[...]
        acc[:, :channels] += part
    col = lax.broadcasted_iota(jnp.int32, (rows, half, 1), 1)
    col = col + (place[3] * (tile_cols // 2) - SIDE // 2)
    keep = (col >= 0) & (col < tile_cols // 2 * col_count)
    value = silu(acc[...]).reshape(rows, half, 2 * LANES)
    value = jnp.where(keep, value, 0.0).reshape(cells, 2 * LANES)
    tail = pltpu.roll(value[:, LANES:], row * 32, 1)
    value = jnp.concatenate([value[:, :LANES], tail], axis=1).astype(BF)
    result[0] = jnp.zeros_like(result[0])
    result[rows + 1] = jnp.zeros_like(result[0])
    result[1 : rows + 1] = value.reshape(rows, half, 2 * LANES)
    for by in range(row_count):
        at = lax.rem(row + by, row_count)
        outs[by][...] = result[pl.ds(tall * at, tall + 2)]


def field_body(sets, place, *refs):
    mids, field = refs[:SHARDS], refs[SHARDS]
    tail = mids[0][:, :, LANES:]
    for mid in mids[1:]:
        tail = tail + mid[:, :, LANES:]
    field[4] = tail
    for by in range(SHARDS):
        shard = lax.rem(place[2] - by + SHARDS, SHARDS) if sets > 1 else by
        field[shard] = mids[by][:, :, :LANES]


def joined_body(size, sets, parts, place, skip, bias, *refs):
    tile_rows, tile_cols = size[:2]
    wide = tile_cols + 2 * SIDE
    field, refs = refs[0], refs[1:]
    sources, refs = refs[:sets], refs[sets:]
    out, weights, shifted, raised, acc, sem = refs
    copies = load_weights(place, parts, sources, weights, sem)
    for copy in copies:
        copy.start()
    spread(skip[...].astype(F32), shifted)
    half = field.shape[2]
    tall = tile_rows // 2 + 2
    cell = lax.broadcasted_iota(jnp.int32, (3 * wide, half), 0)
    move = jnp.where(cell >= 2 * wide, 1 - 2 * wide, jnp.where(cell >= wide, -wide, -1))
    source = lax.broadcasted_iota(jnp.int32, (3 * wide, half), 1)
    place_of = cell + move
    raise_by = jnp.where((place_of >= 2 * source) & (place_of < 2 * source + 2), 1.0, 0.0).astype(BF)
    for row in range(tall):
        block = jnp.concatenate([field[chunk, row] for chunk in range(5)], axis=1)
        up = jnp.dot(raise_by, block, preferred_element_type=F32).astype(BF)
        for dx in range(3):
            for twice in range(2):
                at = (2 * row + twice) * wide
                raised[dx, at : at + wide] = up[dx * wide : (dx + 1) * wide]
    for copy in copies:
        copy.wait()
    rows = tile_rows + 2
    cells = rows * wide
    add_plain(shifted, weights, 0, rows, wide, acc, bias[...])

    def window(tap, first, count):
        return raised[tap % 3, pl.ds((tap // 3) * wide, cells), pl.ds(first, count)]

    for tap in range(9):
        at = 23 + 5 * tap
        for pair in range(2):
            left = window(tap, 256 * pair, 256)
            acc[:cells] += product(left, weight_pair(weights, at + 2 * pair, at + 2 * pair + 1))
        if tap % 2 == 1:
            left = jnp.concatenate([window(tap - 1, 512, LANES), window(tap, 512, LANES)], axis=1)
            acc[:cells] += product(left, weight_pair(weights, at - 1, at + 4))
        elif tap == 8:
            acc[:cells] += product(window(tap, 512, LANES), weight_pair(weights, at + 4, None))
    out[...] = activated(acc, rows, wide, inside(place, rows, wide, -1, -SIDE, size)).astype(BF)


def last_body(size, sets, parts, place, refined, bias, *refs):
    tile_rows, tile_cols = size[:2]
    wide = tile_cols + 2 * SIDE
    sources, refs = refs[:sets], refs[sets:]
    out, weights, shifted, acc, sem = refs
    copies = load_weights(place, parts, sources, weights, sem)
    for copy in copies:
        copy.start()
    spread(refined[...].astype(F32), shifted)
    for copy in copies:
        copy.wait()
    add_plain(shifted, weights, 0, tile_rows, wide, acc, bias[...])
    value = silu(acc[...]).reshape(tile_rows, wide, acc.shape[1])
    out[0] = value[:, SIDE : SIDE + tile_cols, :].astype(BF)


def shards(mesh_shape, latent, enc_first, enc_first_bias, enc_second, enc_second_bias, mid_weight, mid_bias,
           dec_first, dec_first_bias, dec_second, dec_second_bias):
    grps, segs, row_count, col_count = mesh_shape
    grp, seg, row, col = (lax.axis_index(axis) for axis in AXES)
    place = jnp.stack([grp, seg, row, col]).astype(jnp.int32)
    tile_rows, tile_cols, channels = latent.shape[1:]
    size = (tile_rows, tile_cols, row_count, col_count)
    wide = tile_cols + 2 * SIDE
    half = -(-(wide // 2) // 16) * 16
    spread_out = row_count == SHARDS and col_count == 2 and grps == 2 and segs == 2
    plain, joined = plain_chunks(0), joined_chunks()

    groups = (
        ((plain, plain), 8, (enc_first, enc_second)),
        ((joined,), 8, (dec_first,)),
        ((plain,), 8, (dec_second,)),
    )
    if spread_out:
        mine0 = pack_piece(groups[0][0], groups[0][1], place, groups[0][2])
        later = after(place, mine0)
        (own0, _), (own1, mine1), (own2, mine2) = (
            pack(layouts, parts, later, group) for layouts, parts, group in groups
        )

    tile = lax.dynamic_index_in_dim(latent, seg, 0, keepdims=False)
    if spread_out:
        tile = after(tile, mine0)
    down = [(i, i + 1) for i in range(row_count - 1)]
    above = lax.ppermute(tile, "row", down)
    below = lax.ppermute(tile, "row", [(b, a) for a, b in down])
    tile = jnp.concatenate([above, tile, below], axis=0)
    left_edge, right_edge = tile[:, :SIDE], tile[:, tile_cols - SIDE :]
    if col_count == 2:
        edge = lax.ppermute(jnp.where(col == 0, right_edge, left_edge), "col", [(0, 1), (1, 0)])
        blank = jnp.zeros_like(edge)
        left, right = jnp.where(col == 0, blank, edge), jnp.where(col == 0, edge, blank)
    else:
        along = [(i, i + 1) for i in range(col_count - 1)]
        left = lax.ppermute(right_edge, "col", along)
        right = lax.ppermute(left_edge, "col", [(b, a) for a, b in along])
        edge = left
    tile = jnp.concatenate([left, tile, right], axis=1)
    cells = jnp.concatenate([tile, tile[:, :, 256:]], axis=2).reshape(-1, 3 * LANES)

    sets = 5 if spread_out else 1
    weights = []
    if spread_out:
        first, second = plane_moves(mesh_shape)
        across = lambda block, pairs: lax.ppermute(block, AXES, pairs)
        here0 = from_planes(mine0, row_count)
        late = laid(mine1, mine2)
        here1 = from_planes(late, row_count)
        block0 = laid(*after(here0, late, own0))
        block0 = laid(block0, across(block0, first))
        block0 = after(block0, here1[0], above, below)
        far0 = swap_cores(block0)
        next0 = after(across(block0, second), edge, here1[1], here1[2])
        held0 = (block0, next0, far0, swap_cores(next0))
        part1, part2 = mine1.shape[0], mine2.shape[0]
        block1 = laid(*here1, cut=(0, part1))
        weights = [(own0,) + held0]
    else:
        for layouts, parts, group in groups:
            full = [lax.all_gather(weight, "row", axis=2, tiled=True) for weight in group]
            own = pack(layouts, parts, place, full)[0]
            weights.append((own.reshape(own.shape[0], SHARDS, -1, LANES),))

    scratch = lambda *shape: pltpu.VMEM(shape, BF)
    lines = lambda bias: bias.reshape(1, -1)
    packed = lambda source: scratch(source[0].shape[0], SHARDS, channels // SHARDS, LANES)
    skip, pooled = pl.pallas_call(
        functools.partial(encoder_body, size, sets, groups[0][1]),
        out_shape=[
            jax.ShapeDtypeStruct(((tile_rows + 4) * wide, 3 * LANES), BF),
            jax.ShapeDtypeStruct((tile_rows // 2, half, 3 * LANES), BF),
        ],
        in_specs=[SMEM, VMEM, VMEM, VMEM] + [HBM] * sets,
        out_specs=[VMEM, VMEM],
        scratch_shapes=[
            packed(weights[0]),
            scratch(3, 3 * tile_rows * wide, 3 * LANES),
            pltpu.VMEM(((tile_rows + 6) * wide, channels), F32),
            pltpu.SemaphoreType.DMA,
        ],
        compiler_params=params(),
        cost_estimate=cost(4 * (2 * tile_rows + 10) * wide),
        name="encoder",
    )(place, cells, lines(enc_first_bias), lines(enc_second_bias), *weights[0])

    tall = tile_rows // 2
    if spread_out:
        others = [lax.ppermute(pooled, "row", cyclic(row_count, by)) for by in range(1, row_count)]
        block1 = laid(block1, after(across(block1, first), pooled))
        far1 = swap_cores(block1)
        next1 = across(block1, second)
        block2 = laid(*here1, cut=(part1, part2))
        block2 = laid(block2, after(across(block2, first), pooled))
        others = after(others, block2)
        part = mid_weight.shape[2]
        bias = lax.dynamic_slice_in_dim(mid_bias, row * part, part, 0)
        rows = tall * row_count
        sent = pl.pallas_call(
            functools.partial(middle_body, size),
            out_shape=[jax.ShapeDtypeStruct((tall + 2, half, 2 * LANES), BF)] * row_count,
            in_specs=[SMEM] + [VMEM] * (row_count + 2),
            out_specs=[VMEM] * row_count,
            scratch_shapes=[
                pltpu.VMEM((rows + 2, half, 3 * LANES), F32),
                scratch(3, (rows + 2) * half, 3 * LANES),
                pltpu.VMEM((rows * half, 2 * LANES), F32),
                scratch(rows + 2, half, 2 * LANES),
            ],
            compiler_params=params(),
            cost_estimate=cost(4 * tile_rows * wide),
            name="middle",
        )(place, pooled, *others, jnp.swapaxes(mid_weight, 1, 2), lines(bias))
        mids = [sent[0]] + [
            lax.ppermute(sent[by], "row", cyclic(row_count, by)) for by in range(1, row_count)
        ]
        next1 = after(next1, sent[0])
        held1 = (block1, next1, far1, swap_cores(next1))
        next2 = after(across(block2, second), *mids)
        held2 = (block2, next2, swap_cores(block2), swap_cores(next2))
        weights += [(own1,) + held1, (own2,) + held2]
    else:
        full = lax.all_gather(mid_weight, "row", axis=2, tiled=True)
        field = jnp.concatenate(
            [lax.ppermute(pooled, "row", down), pooled, lax.ppermute(pooled, "row", [(b, a) for a, b in down])]
        )[:, :, :channels]
        field = jnp.pad(field, ((0, 0), (1, 1), (0, 0)))
        total = jnp.zeros((tall + 2, half, full.shape[2]), F32)
        first = field.shape[0] // 2 - tall // 2 - 2
        for tap in range(9):
            dy, dx = tap // 3, tap % 3
            window = field[first + dy : first + dy + tall + 2, dx : dx + half]
            total += jnp.einsum("rck,kn->rcn", window, full[tap], preferred_element_type=F32)
        at_row = jnp.arange(tall + 2)[:, None, None] - 1 + row * tall
        at_col = jnp.arange(half)[None, :, None] - SIDE // 2 + col * (tile_cols // 2)
        keep = (at_row >= 0) & (at_row < tall * row_count) & (at_col >= 0) & (at_col < tile_cols // 2 * col_count)
        middle = jnp.where(keep, jax.nn.silu(total + mid_bias), 0.0).astype(BF)
        mids = []
        for shard in range(SHARDS):
            block = middle[:, :, 160 * shard : 160 * (shard + 1)]
            tail = jnp.pad(block[:, :, LANES:], ((0, 0), (0, 0), (32 * shard, 96 - 32 * shard)))
            mids.append(jnp.concatenate([block[:, :, :LANES], tail], axis=2))

    field = pl.pallas_call(
        functools.partial(field_body, sets),
        out_shape=jax.ShapeDtypeStruct((5, tall + 2, half, LANES), BF),
        in_specs=[SMEM] + [VMEM] * SHARDS,
        out_specs=VMEM,
        compiler_params=params(),
        cost_estimate=cost(40 * tile_rows * wide),
        name="field",
    )(place, *mids)
    refined = pl.pallas_call(
        functools.partial(joined_body, size, sets, groups[1][1]),
        out_shape=jax.ShapeDtypeStruct(((tile_rows + 2) * wide, 3 * LANES), BF),
        in_specs=[SMEM, VMEM, VMEM, VMEM] + [HBM] * sets,
        out_specs=VMEM,
        scratch_shapes=[
            packed(weights[1]),
            scratch(3, (tile_rows + 4) * wide, 3 * LANES),
            scratch(3, (tile_rows + 4) * wide, 5 * LANES),
            pltpu.VMEM(((tile_rows + 2) * wide, channels), F32),
            pltpu.SemaphoreType.DMA,
        ],
        compiler_params=params(),
        cost_estimate=cost(6 * (tile_rows + 2) * wide),
        name="joined",
    )(place, skip, lines(dec_first_bias), field, *weights[1])
    return pl.pallas_call(
        functools.partial(last_body, size, sets, groups[2][1]),
        out_shape=jax.ShapeDtypeStruct((1, tile_rows, tile_cols, channels), BF),
        in_specs=[SMEM, VMEM, VMEM] + [HBM] * sets,
        out_specs=VMEM,
        scratch_shapes=[
            packed(weights[2]),
            scratch(3, (tile_rows + 2) * wide, 3 * LANES),
            pltpu.VMEM((tile_rows * wide, channels), F32),
            pltpu.SemaphoreType.DMA,
        ],
        compiler_params=params(),
        cost_estimate=cost(2 * tile_rows * wide),
        name="last",
    )(place, refined, lines(dec_second_bias), *weights[2])


def solution(mesh):
    placed = (
        P("grp", "row", "col", None),
        P(None, None, "row"),
        P(),
        P(None, None, "row"),
        P(),
        P(None, None, "row"),
        P(),
        P(None, None, "row"),
        P(),
        P(None, None, "row"),
        P(),
    )
    mesh_shape = tuple(mesh.shape[axis] for axis in AXES)
    return jax.shard_map(
        functools.partial(shards, mesh_shape),
        mesh=mesh,
        in_specs=placed,
        out_specs=P(("grp", "segment"), "row", "col", None),
        check_vma=False,
    )
```

```python
import functools

import jax
import jax.numpy as jnp
from jax import lax
from jax.experimental import pallas as pl
from jax.experimental.pallas import tpu as pltpu
from jax.sharding import PartitionSpec as P

BF = jnp.bfloat16
F32 = jnp.float32
LANES = 128
SIDE = 8
AXES = ("grp", "segment", "row", "col")
PIECES = 8
SHARDS = 4
VMEM = pl.BlockSpec(memory_space=pltpu.VMEM)
HBM = pl.BlockSpec(memory_space=pl.ANY)
SMEM = pl.BlockSpec(memory_space=pltpu.SMEM)


def params():
    return pltpu.CompilerParams(vmem_limit_bytes=36 * 1024 * 1024)


def cost(cells):
    return pl.CostEstimate(flops=cells * 9 * 320 * 640 * 2, bytes_accessed=1 << 20, transcendentals=0)


def plain_chunks(base):
    chunks = [[(tap, base + half * LANES, LANES)] for tap in range(9) for half in range(2)]
    rest = [(tap, base + 256, 64) for tap in range(9)]
    for at in range(0, 9, 2):
        chunks.append(rest[at : at + 2])
    return chunks


def joined_chunks():
    chunks = plain_chunks(0)
    for tap in range(9):
        for shard in range(4):
            chunks.append([(tap, 320 + shard * 160, LANES)])
        chunks.append([(tap, 320 + shard * 160 + LANES, 32) for shard in range(4)])
    return chunks


def padded_count(chunks):
    return -(-len(chunks) // PIECES) * PIECES


def pack_body(layouts, parts, place, *refs):
    count = len(layouts)
    own, mine = refs[count:]
    index = 0
    for chunks, source in zip(layouts, refs):
        channels = source.shape[1]
        for chunk in chunks:
            parts = [source[tap, :, pl.ds(first, size)] for tap, first, size in chunk]
            have = sum(part.shape[1] for part in parts)
            if have < LANES:
                parts.append(jnp.zeros((channels, LANES - have), BF))
            own[index] = parts[0] if len(parts) == 1 else jnp.concatenate(parts, axis=1)
            index += 1
    while index < own.shape[0]:
        own[index] = jnp.zeros(own.shape[1:], BF)
        index += 1
    size = mine.shape[0]
    mine[...] = own[pl.ds(owner_piece(place, parts, place[1], 0) * size, size)]


def pack(layouts, parts, place, weights):
    total = padded_count([chunk for chunks in layouts for chunk in chunks])
    weights = [jnp.swapaxes(weight, 1, 2) for weight in weights]
    channels = weights[0].shape[1]
    return pl.pallas_call(
        functools.partial(pack_body, layouts, parts),
        out_shape=[
            jax.ShapeDtypeStruct((total, channels, LANES), BF),
            jax.ShapeDtypeStruct((total // parts, channels, LANES), BF),
        ],
        in_specs=[SMEM] + [VMEM] * len(weights),
        out_specs=[VMEM, VMEM],
        compiler_params=params(),
        name="pack_weights",
    )(place, *weights)


def piece_body(layouts, parts, place, *refs):
    count = len(layouts)
    sources, mine, held, sems = refs[:count], refs[count], refs[count + 1 : -1], refs[-1]
    copies = [pltpu.make_async_copy(a, b, sems.at[i]) for i, (a, b) in enumerate(zip(sources, held))]
    for copy in copies:
        copy.start()
    for copy in copies:
        copy.wait()
    chunks = [(source, chunk) for source, layer in zip(held, layouts) for chunk in layer]
    size, channels = mine.shape[:2]
    wanted = owner_piece(place, parts, place[1], 0)
    for piece in range(parts):

        @pl.when(wanted == piece)
        def _(piece=piece):
            for index in range(size):
                block = [jnp.zeros((channels, LANES), BF)]
                if piece * size + index < len(chunks):
                    source, chunk = chunks[piece * size + index]
                    block = [source[tap, :, pl.ds(first, width)] for tap, first, width in chunk]
                    have = sum(part.shape[1] for part in block)
                    if have < LANES:
                        block.append(jnp.zeros((channels, LANES - have), BF))
                mine[index] = block[0] if len(block) == 1 else jnp.concatenate(block, axis=1)


def pack_piece(layouts, parts, place, weights):
    total = padded_count([chunk for chunks in layouts for chunk in chunks])
    weights = [jnp.swapaxes(weight, 1, 2) for weight in weights]
    return pl.pallas_call(
        functools.partial(piece_body, layouts, parts),
        out_shape=jax.ShapeDtypeStruct((total // parts, weights[0].shape[1], LANES), BF),
        in_specs=[SMEM] + [HBM] * len(weights),
        out_specs=VMEM,
        scratch_shapes=[pltpu.VMEM(weight.shape, BF) for weight in weights]
        + [pltpu.SemaphoreType.DMA((len(weights),))],
        compiler_params=pltpu.CompilerParams(vmem_limit_bytes=36 * 1024 * 1024),
        name="pack_piece",
    )(place, *weights)


def device_pairs(mesh_shape, move):
    grps, segs, rows, cols = mesh_shape
    place = lambda g, s, r, c: ((g * segs + s) * rows + r) * cols + c
    return [
        (place(g, s, r, c), place(*move(g, s, r, c)))
        for g in range(grps)
        for s in range(segs)
        for r in range(rows)
        for c in range(cols)
    ]


def cyclic(count, by):
    return [(i, (i + by) % count) for i in range(count)]


def after(value, *others):
    return lax.optimization_barrier((value,) + others)[0]


def laid_body(cuts, *refs):
    count = len(cuts)
    sources, target, sems = refs[:count], refs[count], refs[count + 1]
    copies, at = [], 0
    for index, (source, (first, size)) in enumerate(zip(sources, cuts)):
        copies.append(
            pltpu.make_async_copy(
                source.at[pl.ds(first, size)], target.at[pl.ds(at, size)], sems.at[index]
            )
        )
        at += size
    for copy in copies:
        copy.start()
    for copy in copies:
        copy.wait()


def laid(*parts, cut=None):
    cuts = tuple(cut or (0, part.shape[0]) for part in parts)
    return pl.pallas_call(
        functools.partial(laid_body, cuts),
        out_shape=jax.ShapeDtypeStruct((sum(size for _, size in cuts),) + parts[0].shape[1:], BF),
        in_specs=[HBM] * len(parts),
        out_specs=VMEM,
        scratch_shapes=[pltpu.SemaphoreType.DMA((len(parts),))],
        compiler_params=params(),
        cost_estimate=pl.CostEstimate(flops=0, bytes_accessed=1 << 21, transcendentals=0),
        name="laid",
    )(*parts)


def from_planes(mine, count):
    return [lax.ppermute(mine, "row", cyclic(count, by)) for by in range(1, count)]


def plane_moves(mesh_shape):
    first = device_pairs(
        mesh_shape, lambda g, s, r, c: (g, s, r, 1 - c) if s == 0 else (1 - g, s, r, c)
    )
    second = device_pairs(
        mesh_shape, lambda g, s, r, c: (1 - g, s, r, c) if s == 0 else (g, s, r, 1 - c)
    )
    return first, second


def swap_cores(block):
    return lax.ppermute(block, "segment", [(0, 1), (1, 0)])


def owner_piece(place, parts, core, slot):
    grp, col = place[0], place[3]
    low, high = slot % 2, slot // 2
    if parts == 4:
        col, grp = (1 - col, 1 - grp) if low else (col, grp)
        return jnp.where(core == 0, col, 2 + grp)
    flip_col = jnp.where(core == 0, low, high)
    flip_grp = jnp.where(core == 0, high, low)
    grp = jnp.where(flip_grp == 1, 1 - grp, grp)
    col = jnp.where(flip_col == 1, 1 - col, col)
    return (grp * 2 + core) * 2 + col


def load_weights(place, parts, sources, target, sem):
    if len(sources) == 1:
        return [pltpu.make_async_copy(sources[0], target, sem)]
    own, near0, near1, far0, far1 = sources
    seg, row = place[1], place[2]
    size = own.shape[0] // parts
    each = parts // 4
    copies = [pltpu.make_async_copy(own, target.at[:, row], sem)]
    for pair, core in (((near0, near1), seg), ((far0, far1), 1 - seg)):
        for slot in range(2 * each):
            array = pair[slot // each]
            piece = owner_piece(place, parts, core, slot)
            for by in range(1, SHARDS):
                shard = lax.rem(row - by + SHARDS, SHARDS)
                source = array.at[pl.ds(((slot % each) * 3 + by - 1) * size, size)]
                copies.append(
                    pltpu.make_async_copy(source, target.at[pl.ds(piece * size, size), shard], sem)
                )
    return copies


def silu(value):
    return value / (1.0 + jnp.exp(-value))


def spread(value, shifted):
    cells = value.shape[0]
    shifted[0, :cells] = pltpu.roll(value, 1, 0).astype(BF)
    shifted[1, :cells] = value.astype(BF)
    shifted[2, :cells] = pltpu.roll(value, cells - 1, 0).astype(BF)


def weight_pair(weights, low, high):
    parts = []
    for index in (low, high):
        if index is not None:
            block = weights[index]
            parts.append(block.reshape(block.shape[0] * block.shape[1], LANES))
    return parts[0] if len(parts) == 1 else jnp.concatenate(parts, axis=1)


def product(left, right):
    return lax.dot_general(left, right, (((1,), (1,)), ((), ())), preferred_element_type=F32)


def add_plain(shifted, weights, base, rows, wide, acc, bias):
    cells = rows * wide

    def window(tap, first, size):
        at = (tap // 3) * wide
        return shifted[tap % 3, pl.ds(at, cells), pl.ds(first, size)]

    def rest(at):
        low = window(2 * at, 256, LANES)
        if at == 4:
            return low
        high = window(2 * at + 1, 256, LANES)
        lane = lax.broadcasted_iota(jnp.int32, (cells, LANES), 1)
        return jnp.where(lane < 64, low, high)

    acc[:cells] = product(window(0, 0, 256), weight_pair(weights, base, base + 1)) + bias
    for tap in range(1, 9):
        acc[:cells] += product(window(tap, 0, 256), weight_pair(weights, base + 2 * tap, base + 2 * tap + 1))
    for at in range(0, 4, 2):
        left = jnp.concatenate([rest(at), rest(at + 1)], axis=1)
        acc[:cells] += product(left, weight_pair(weights, base + 18 + at, base + 19 + at))
    acc[:cells] += product(rest(4), weight_pair(weights, base + 22, None))


def inside(place, rows, wide, first_row, first_col, size):
    tile_rows, tile_cols, row_count, col_count = size
    row = lax.broadcasted_iota(jnp.int32, (rows, wide, 1), 0) + (place[2] * tile_rows + first_row)
    col = lax.broadcasted_iota(jnp.int32, (rows, wide, 1), 1) + (place[3] * tile_cols + first_col)
    return (row >= 0) & (row < tile_rows * row_count) & (col >= 0) & (col < tile_cols * col_count)


def activated(acc, rows, wide, keep):
    value = silu(acc[: rows * wide]).reshape(rows, wide, acc.shape[1])
    value = jnp.where(keep, value, 0.0).reshape(rows * wide, acc.shape[1])
    value = value.astype(BF).astype(F32)
    return jnp.concatenate([value, value[:, 256:320]], axis=1)


def encoder_body(size, sets, parts, place, cells, bias1, bias2, *refs):
    tile_rows, tile_cols = size[:2]
    wide = tile_cols + 2 * SIDE
    sources, refs = refs[:sets], refs[sets:]
    skip, pooled, weights, shifted, acc, sem = refs
    copies = load_weights(place, parts, sources, weights, sem)
    for copy in copies:
        copy.start()
    spread(cells[...].astype(F32), shifted)
    for copy in copies:
        copy.wait()
    rows = tile_rows + 6
    add_plain(shifted, weights, 0, rows, wide, acc, bias1[...])
    hidden = activated(acc, rows, wide, inside(place, rows, wide, -3, -SIDE, size))
    spread(hidden, shifted)
    rows = tile_rows + 4
    add_plain(shifted, weights, 23, rows, wide, acc, bias2[...])
    value = activated(acc, rows, wide, inside(place, rows, wide, -2, -SIDE, size)).astype(BF)
    skip[...] = value
    half = pooled.shape[1]
    cell = lax.broadcasted_iota(jnp.int32, (half, 2 * wide), 1)
    cell = jnp.where(cell >= wide, cell - wide, cell)
    target = lax.broadcasted_iota(jnp.int32, (half, 2 * wide), 0)
    mean = jnp.where(cell // 2 == target, 0.25, 0.0).astype(BF)
    for row in range(tile_rows // 2):
        at = (2 + 2 * row) * wide
        block = value[at : at + 2 * wide]
        pooled[row] = jnp.dot(mean, block, preferred_element_type=F32).astype(BF)


def middle_body(size, place, own, *refs):
    tile_rows, tile_cols, row_count, col_count = size
    others, refs = refs[: row_count - 1], refs[row_count - 1 :]
    weights, bias = refs[:2]
    outs, refs = refs[2 : 2 + row_count], refs[2 + row_count :]
    field, shifted, acc, result = refs
    row = place[2]
    tall, half = tile_rows // 2, own.shape[1]
    rows = tall * row_count
    flat = (rows + 2) * half
    field[0] = jnp.zeros_like(field[0])
    field[rows + 1] = jnp.zeros_like(field[0])
    for by in range(row_count):
        source = own if by == 0 else others[by - 1]
        at = lax.rem(row - by + row_count, row_count)
        field[pl.ds(1 + tall * at, tall)] = source[...].astype(F32)
    spread(field[...].reshape(flat, field.shape[2]), shifted)
    cells = rows * half
    channels = weights.shape[1]
    acc[...] = jnp.zeros_like(acc)
    for tap in range(9):
        at = (tap // 3) * half
        left = shifted[tap % 3, pl.ds(at, cells), :]
        part = product(left[:, :256], weights[tap, :, :256])
        part += product(left[:, 256:320], weights[tap, :, 256:320])
        if tap == 0:
            part += bias[...]
        acc[:, :channels] += part
    col = lax.broadcasted_iota(jnp.int32, (rows, half, 1), 1)
    col = col + (place[3] * (tile_cols // 2) - SIDE // 2)
    keep = (col >= 0) & (col < tile_cols // 2 * col_count)
    value = silu(acc[...]).reshape(rows, half, 2 * LANES)
    value = jnp.where(keep, value, 0.0).reshape(cells, 2 * LANES)
    tail = pltpu.roll(value[:, LANES:], row * 32, 1)
    value = jnp.concatenate([value[:, :LANES], tail], axis=1).astype(BF)
    result[0] = jnp.zeros_like(result[0])
    result[rows + 1] = jnp.zeros_like(result[0])
    result[1 : rows + 1] = value.reshape(rows, half, 2 * LANES)
    for by in range(row_count):
        at = lax.rem(row + by, row_count)
        outs[by][...] = result[pl.ds(tall * at, tall + 2)]


def field_body(sets, place, *refs):
    mids, field = refs[:SHARDS], refs[SHARDS]
    tail = mids[0][:, :, LANES:]
    for mid in mids[1:]:
        tail = tail + mid[:, :, LANES:]
    field[4] = tail
    for by in range(SHARDS):
        shard = lax.rem(place[2] - by + SHARDS, SHARDS) if sets > 1 else by
        field[shard] = mids[by][:, :, :LANES]


def joined_body(size, sets, parts, place, skip, bias, *refs):
    tile_rows, tile_cols = size[:2]
    wide = tile_cols + 2 * SIDE
    field, refs = refs[0], refs[1:]
    sources, refs = refs[:sets], refs[sets:]
    out, weights, shifted, raised, acc, sem = refs
    copies = load_weights(place, parts, sources, weights, sem)
    for copy in copies:
        copy.start()
    spread(skip[...].astype(F32), shifted)
    half = field.shape[2]
    tall = tile_rows // 2 + 2
    cell = lax.broadcasted_iota(jnp.int32, (3 * wide, half), 0)
    move = jnp.where(cell >= 2 * wide, 1 - 2 * wide, jnp.where(cell >= wide, -wide, -1))
    source = lax.broadcasted_iota(jnp.int32, (3 * wide, half), 1)
    place_of = cell + move
    raise_by = jnp.where((place_of >= 2 * source) & (place_of < 2 * source + 2), 1.0, 0.0).astype(BF)
    for row in range(tall):
        block = jnp.concatenate([field[chunk, row] for chunk in range(5)], axis=1)
        up = jnp.dot(raise_by, block, preferred_element_type=F32).astype(BF)
        for dx in range(3):
            for twice in range(2):
                at = (2 * row + twice) * wide
                raised[dx, at : at + wide] = up[dx * wide : (dx + 1) * wide]
    for copy in copies:
        copy.wait()
    rows = tile_rows + 2
    cells = rows * wide
    add_plain(shifted, weights, 0, rows, wide, acc, bias[...])

    def window(tap, first, count):
        return raised[tap % 3, pl.ds((tap // 3) * wide, cells), pl.ds(first, count)]

    for tap in range(9):
        at = 23 + 5 * tap
        for pair in range(2):
            left = window(tap, 256 * pair, 256)
            acc[:cells] += product(left, weight_pair(weights, at + 2 * pair, at + 2 * pair + 1))
        if tap % 2 == 1:
            left = jnp.concatenate([window(tap - 1, 512, LANES), window(tap, 512, LANES)], axis=1)
            acc[:cells] += product(left, weight_pair(weights, at - 1, at + 4))
        elif tap == 8:
            acc[:cells] += product(window(tap, 512, LANES), weight_pair(weights, at + 4, None))
    out[...] = activated(acc, rows, wide, inside(place, rows, wide, -1, -SIDE, size)).astype(BF)


def last_body(size, sets, parts, place, refined, bias, *refs):
    tile_rows, tile_cols = size[:2]
    wide = tile_cols + 2 * SIDE
    sources, refs = refs[:sets], refs[sets:]
    out, weights, shifted, acc, sem = refs
    copies = load_weights(place, parts, sources, weights, sem)
    for copy in copies:
        copy.start()
    spread(refined[...].astype(F32), shifted)
    for copy in copies:
        copy.wait()
    add_plain(shifted, weights, 0, tile_rows, wide, acc, bias[...])
    value = silu(acc[...]).reshape(tile_rows, wide, acc.shape[1])
    out[0] = value[:, SIDE : SIDE + tile_cols, :].astype(BF)


def shards(mesh_shape, latent, enc_first, enc_first_bias, enc_second, enc_second_bias, mid_weight, mid_bias,
           dec_first, dec_first_bias, dec_second, dec_second_bias):
    grps, segs, row_count, col_count = mesh_shape
    grp, seg, row, col = (lax.axis_index(axis) for axis in AXES)
    place = jnp.stack([grp, seg, row, col]).astype(jnp.int32)
    tile_rows, tile_cols, channels = latent.shape[1:]
    size = (tile_rows, tile_cols, row_count, col_count)
    wide = tile_cols + 2 * SIDE
    half = -(-(wide // 2) // 16) * 16
    spread_out = row_count == SHARDS and col_count == 2 and grps == 2 and segs == 2
    plain, joined = plain_chunks(0), joined_chunks()

    groups = (
        ((plain, plain), 8, (enc_first, enc_second)),
        ((joined,), 8, (dec_first,)),
        ((plain,), 8, (dec_second,)),
    )
    if spread_out:
        mine0 = pack_piece(groups[0][0], groups[0][1], place, groups[0][2])
        later = after(place, mine0)
        (own0, _), (own1, mine1), (own2, mine2) = (
            pack(layouts, parts, later, group) for layouts, parts, group in groups
        )

    tile = lax.dynamic_index_in_dim(latent, seg, 0, keepdims=False)
    if spread_out:
        tile = after(tile, mine0)
    down = [(i, i + 1) for i in range(row_count - 1)]
    above = lax.ppermute(tile, "row", down)
    below = lax.ppermute(tile, "row", [(b, a) for a, b in down])
    tile = jnp.concatenate([above, tile, below], axis=0)
    left_edge, right_edge = tile[:, :SIDE], tile[:, tile_cols - SIDE :]
    if col_count == 2:
        edge = lax.ppermute(jnp.where(col == 0, right_edge, left_edge), "col", [(0, 1), (1, 0)])
        blank = jnp.zeros_like(edge)
        left, right = jnp.where(col == 0, blank, edge), jnp.where(col == 0, edge, blank)
    else:
        along = [(i, i + 1) for i in range(col_count - 1)]
        left = lax.ppermute(right_edge, "col", along)
        right = lax.ppermute(left_edge, "col", [(b, a) for a, b in along])
        edge = left
    tile = jnp.concatenate([left, tile, right], axis=1)
    cells = jnp.concatenate([tile, tile[:, :, 256:]], axis=2).reshape(-1, 3 * LANES)

    sets = 5 if spread_out else 1
    weights = []
    if spread_out:
        first, second = plane_moves(mesh_shape)
        across = lambda block, pairs: lax.ppermute(block, AXES, pairs)
        here0 = from_planes(mine0, row_count)
        late = laid(mine1, mine2)
        here1 = from_planes(late, row_count)
        block0 = laid(*after(here0, late, own0))
        block0 = laid(block0, across(block0, first))
        block0 = after(block0, here1[0], above, below)
        far0 = swap_cores(block0)
        next0 = after(across(block0, second), edge, here1[1], here1[2])
        held0 = (block0, next0, far0, swap_cores(next0))
        part1, part2 = mine1.shape[0], mine2.shape[0]
        block1 = laid(*here1, cut=(0, part1))
        weights = [(own0,) + held0]
    else:
        for layouts, parts, group in groups:
            full = [lax.all_gather(weight, "row", axis=2, tiled=True) for weight in group]
            own = pack(layouts, parts, place, full)[0]
            weights.append((own.reshape(own.shape[0], SHARDS, -1, LANES),))

    scratch = lambda *shape: pltpu.VMEM(shape, BF)
    lines = lambda bias: bias.reshape(1, -1)
    packed = lambda source: scratch(source[0].shape[0], SHARDS, channels // SHARDS, LANES)
    skip, pooled = pl.pallas_call(
        functools.partial(encoder_body, size, sets, groups[0][1]),
        out_shape=[
            jax.ShapeDtypeStruct(((tile_rows + 4) * wide, 3 * LANES), BF),
            jax.ShapeDtypeStruct((tile_rows // 2, half, 3 * LANES), BF),
        ],
        in_specs=[SMEM, VMEM, VMEM, VMEM] + [HBM] * sets,
        out_specs=[VMEM, VMEM],
        scratch_shapes=[
            packed(weights[0]),
            scratch(3, 3 * tile_rows * wide, 3 * LANES),
            pltpu.VMEM(((tile_rows + 6) * wide, channels), F32),
            pltpu.SemaphoreType.DMA,
        ],
        compiler_params=params(),
        cost_estimate=cost(4 * (2 * tile_rows + 10) * wide),
        name="encoder",
    )(place, cells, lines(enc_first_bias), lines(enc_second_bias), *weights[0])

    tall = tile_rows // 2
    if spread_out:
        others = [lax.ppermute(pooled, "row", cyclic(row_count, by)) for by in range(1, row_count)]
        block1 = laid(block1, after(across(block1, first), pooled))
        far1 = swap_cores(block1)
        next1 = across(block1, second)
        block2 = laid(*here1, cut=(part1, part2))
        block2 = laid(block2, after(across(block2, first), pooled))
        part = mid_weight.shape[2]
        bias = lax.dynamic_slice_in_dim(mid_bias, row * part, part, 0)
        rows = tall * row_count
        sent = pl.pallas_call(
            functools.partial(middle_body, size),
            out_shape=[jax.ShapeDtypeStruct((tall + 2, half, 2 * LANES), BF)] * row_count,
            in_specs=[SMEM] + [VMEM] * (row_count + 2),
            out_specs=[VMEM] * row_count,
            scratch_shapes=[
                pltpu.VMEM((rows + 2, half, 3 * LANES), F32),
                scratch(3, (rows + 2) * half, 3 * LANES),
                pltpu.VMEM((rows * half, 2 * LANES), F32),
                scratch(rows + 2, half, 2 * LANES),
            ],
            compiler_params=params(),
            cost_estimate=cost(4 * tile_rows * wide),
            name="middle",
        )(place, pooled, *others, jnp.swapaxes(mid_weight, 1, 2), lines(bias))
        mids = [sent[0]] + [
            lax.ppermute(sent[by], "row", cyclic(row_count, by)) for by in range(1, row_count)
        ]
        next1 = after(next1, sent[0], block2)
        held1 = (block1, next1, far1, swap_cores(next1))
        next2 = after(across(block2, second), *mids)
        held2 = (block2, next2, swap_cores(block2), swap_cores(next2))
        weights += [(own1,) + held1, (own2,) + held2]
    else:
        full = lax.all_gather(mid_weight, "row", axis=2, tiled=True)
        field = jnp.concatenate(
            [lax.ppermute(pooled, "row", down), pooled, lax.ppermute(pooled, "row", [(b, a) for a, b in down])]
        )[:, :, :channels]
        field = jnp.pad(field, ((0, 0), (1, 1), (0, 0)))
        total = jnp.zeros((tall + 2, half, full.shape[2]), F32)
        first = field.shape[0] // 2 - tall // 2 - 2
        for tap in range(9):
            dy, dx = tap // 3, tap % 3
            window = field[first + dy : first + dy + tall + 2, dx : dx + half]
            total += jnp.einsum("rck,kn->rcn", window, full[tap], preferred_element_type=F32)
        at_row = jnp.arange(tall + 2)[:, None, None] - 1 + row * tall
        at_col = jnp.arange(half)[None, :, None] - SIDE // 2 + col * (tile_cols // 2)
        keep = (at_row >= 0) & (at_row < tall * row_count) & (at_col >= 0) & (at_col < tile_cols // 2 * col_count)
        middle = jnp.where(keep, jax.nn.silu(total + mid_bias), 0.0).astype(BF)
        mids = []
        for shard in range(SHARDS):
            block = middle[:, :, 160 * shard : 160 * (shard + 1)]
            tail = jnp.pad(block[:, :, LANES:], ((0, 0), (0, 0), (32 * shard, 96 - 32 * shard)))
            mids.append(jnp.concatenate([block[:, :, :LANES], tail], axis=2))

    field = pl.pallas_call(
        functools.partial(field_body, sets),
        out_shape=jax.ShapeDtypeStruct((5, tall + 2, half, LANES), BF),
        in_specs=[SMEM] + [VMEM] * SHARDS,
        out_specs=VMEM,
        compiler_params=params(),
        cost_estimate=cost(40 * tile_rows * wide),
        name="field",
    )(place, *mids)
    refined = pl.pallas_call(
        functools.partial(joined_body, size, sets, groups[1][1]),
        out_shape=jax.ShapeDtypeStruct(((tile_rows + 2) * wide, 3 * LANES), BF),
        in_specs=[SMEM, VMEM, VMEM, VMEM] + [HBM] * sets,
        out_specs=VMEM,
        scratch_shapes=[
            packed(weights[1]),
            scratch(3, (tile_rows + 4) * wide, 3 * LANES),
            scratch(3, (tile_rows + 4) * wide, 5 * LANES),
            pltpu.VMEM(((tile_rows + 2) * wide, channels), F32),
            pltpu.SemaphoreType.DMA,
        ],
        compiler_params=params(),
        cost_estimate=cost(6 * (tile_rows + 2) * wide),
        name="joined",
    )(place, skip, lines(dec_first_bias), field, *weights[1])
    return pl.pallas_call(
        functools.partial(last_body, size, sets, groups[2][1]),
        out_shape=jax.ShapeDtypeStruct((1, tile_rows, tile_cols, channels), BF),
        in_specs=[SMEM, VMEM, VMEM] + [HBM] * sets,
        out_specs=VMEM,
        scratch_shapes=[
            packed(weights[2]),
            scratch(3, (tile_rows + 2) * wide, 3 * LANES),
            pltpu.VMEM((tile_rows * wide, channels), F32),
            pltpu.SemaphoreType.DMA,
        ],
        compiler_params=params(),
        cost_estimate=cost(2 * tile_rows * wide),
        name="last",
    )(place, refined, lines(dec_second_bias), *weights[2])


def solution(mesh):
    placed = (
        P("grp", "row", "col", None),
        P(None, None, "row"),
        P(),
        P(None, None, "row"),
        P(),
        P(None, None, "row"),
        P(),
        P(None, None, "row"),
        P(),
        P(None, None, "row"),
        P(),
    )
    mesh_shape = tuple(mesh.shape[axis] for axis in AXES)
    return jax.shard_map(
        functools.partial(shards, mesh_shape),
        mesh=mesh,
        in_specs=placed,
        out_specs=P(("grp", "segment"), "row", "col", None),
        check_vma=False,
    )
```
